32 devices in a mesh: lat: 4 (over y, x), lon: 8 (over z, core).
Axes of the slice: x: 2, y: 2, z: 4, core: 2. Of those that a mesh axis runs over, the one named last changes fastest.
Arguments:
- tide_state: float32 [48, 512, 1024], P(None, 'lat', 'lon'), may hold values from -6 to 6
- potential: float32 [48, 512, 1024], P(None, 'lat', 'lon'), may hold values from -6 to 6
- water_depth: float32 [512, 1024], P('lat', 'lon'), may hold values from 0.1 to 1
- drag_coeff: float32 [512, 1024], P('lat', 'lon'), may hold values from 0.1 to 2
- ocean_mask: int32 [512, 1024], P('lat', 'lon'), may hold values 0 or 1
- residual_rows: float32 [16, 1048576], P(None, ('lat', 'lon')), may hold values from -6 to 6
- dest_tile: int32 [1048576, 1], P(('lat', 'lon')), may hold values from 0 to 7; in each aligned block of 32768 rows (0 to 32767, 32768 to 65535, ...) at most 8192 rows name the same one
- dest_cell: int32 [1048576], P(('lat', 'lon')), may hold values from 0 to 16383
Outputs:
- tide_field: float32 [48, 512, 1024], P(None, 'lat', 'lon')
The draws below stay inside these ranges and needn't reach their ends.
Inputs may be any that keep to these rules, and one draw needn't show every extreme that they name: `dest_tile`: the rows of one device name each longitude tile at most 8192 times, a bound that some block reaches.
All inputs are finite; a program needn't handle non-finite values. No bound on the sum of `ocean_mask` on one device may be relied on, other than what follows from the above.
Results may differ from the reference program's by a relative error of at most 0.00002.
Values sent between devices are 32-bit elements; how exact they have to be, the bound alone decides.
No kernel may reach another device: no remote copies, remote signals or barrier semaphores. Data moves between devices by JAX's collectives and lax.ppermute only.
A program may use at most 192 MiB of HBM per device.

```python
import math
import jax
import jax.numpy as jnp
import numpy as np
from jax import lax

CLAT = 128
CLON = 128
ROWS_DEV = 32768
CONSTS = 8
SWEEPS = 3
FIELDS = 48
ROW_W = 16
CAP = 8192
NLAT = 512
NLON = 1024
ROWS = 1048576
N_LON = 8


def touch_ends(array, own_key, low, largest):
    shape = array.shape
    index_at = [jax.random.randint(jax.random.fold_in(own_key, axis), (), 0, shape[axis]) for axis in range(len(shape))]
    array = array.at[tuple(index_at)].set(low)
    longest = shape.index(max(shape))
    index_at[longest] = (index_at[longest] + 1) % shape[longest]
    return array.at[tuple(index_at)].set(largest)


def level_of(own_key, shape, cuts, low, largest):
    level = 1.0
    for axis_at, blocks in cuts:
        draws = jax.random.uniform(jax.random.fold_in(jax.random.fold_in(own_key, 6), axis_at), (blocks,), jnp.float32, low / len(cuts), largest / len(cuts))
        level = level * jnp.repeat(jnp.exp(draws), shape[axis_at] // blocks).reshape((-1,) + (1,) * (len(shape) - 1 - axis_at))
    return level


def deal_out(own_key, own, number, rows, amount, top, reach, lean):
    ranking = jax.random.permutation(own_key, amount)
    heavy_load, usual = load_shares(amount, rows * top, reach, lean, True), load_shares(amount, rows * top, reach, lean, False)
    places = jnp.arange(amount)

    def named(tallies, offset_by):
        used = int((tallies > 0).sum())
        fixed = max(1, used // 4)
        moved = fixed + (places - fixed + offset_by * (used - fixed)) % max(1, amount - fixed)
        return jnp.zeros((amount,), jnp.int32).at[ranking[jnp.where(places < fixed, places, moved)]].set(jnp.asarray(tallies, jnp.int32))

    tallies = jnp.where(number % 4 == 0, named(heavy_load, number // 4), named(usual, number - number // 4 - 1))
    mixed = jax.random.permutation(jax.random.fold_in(own, 3), amount)
    donor, receiver = mixed[0:amount // 2 * 2:2], mixed[1:amount // 2 * 2:2]
    room = jnp.minimum(tallies[donor] - 1, reach - tallies[receiver]) // 2
    room = jnp.where((donor == ranking[0]) | (receiver == ranking[0]) | (tallies[receiver] == 0), 0, jnp.maximum(room, 0))
    moved = jax.random.randint(jax.random.fold_in(own, 4), (amount // 2,), 0, 1 << 20) % (room + 1)
    tallies = tallies.at[donor].add(-moved).at[receiver].add(moved)
    items = jnp.searchsorted(jnp.cumsum(tallies), jnp.arange(rows * top), side="right").astype(jnp.int32)
    grid = items.reshape(top, rows).T
    grid = grid[jax.random.permutation(jax.random.fold_in(own, 1), rows)]
    offset_by = jax.random.randint(jax.random.fold_in(own, 2), (rows, 1), 0, top)
    return jnp.take_along_axis(grid, (jnp.arange(top)[None, :] + offset_by) % top, axis=1)


def load_shares(count, total, reach, lean, full):
    loads = [(1 << 20) // math.isqrt(rank ** lean) + 1 for rank in range(1, count + 1)]
    largest = reach if full else min(reach, max(-(-total // count), total * loads[0] // sum(loads)))
    least = 1 if total - largest >= count - 1 else 0
    given, spare = [largest] + [least] * (count - 1), total - largest - least * (count - 1)
    while spare > 0:
        movable = [i for i in range(1, count) if given[i] < largest] or [i for i in range(1, count) if given[i] < reach]
        pool, remaining = sum([loads[i] for i in movable]), spare
        for i in movable:
            extra = min(reach - given[i], max(1, remaining * loads[i] // pool), spare)
            given[i] = given[i] + extra
            spare = spare - extra
    return np.array(given)


def centred(stream_key, shape, deviation, most, shards=(), held_as=jnp.bfloat16):
    drawn = jax.random.normal(stream_key, shape, jnp.float32) * deviation
    if len(shards) > 0:
        drawn = level_of(stream_key, shape, shards, -0.22, 0.18) * drawn
    return jnp.clip(drawn, min=-most, max=most).astype(held_as)


def setup_inputs(seed: int = 0) -> dict:
    keys = jax.random.split(jax.random.key(seed), 9)
    tide_state = centred(keys[0], (FIELDS, NLAT, NLON), 1.0, 6.0, ((1, 4), (2, 8)), jnp.float32)
    potential = centred(keys[1], (FIELDS, NLAT, NLON), 1.0, 6.0, ((1, 4), (2, 8)), jnp.float32)
    water_depth = jnp.clip(jnp.exp(math.log(1.0) - 2.3025851 * jax.random.uniform(keys[2], (NLAT, NLON), jnp.float32) ** level_of(keys[2], (NLAT, NLON), ((0, 4), (1, 8)), -0.2, 0.2)), 0.1, 1.0)
    drag_coeff = jnp.clip(jnp.exp(math.log(2.0) - 2.9957323 * jax.random.uniform(keys[3], (NLAT, NLON), jnp.float32) ** level_of(keys[3], (NLAT, NLON), ((0, 4), (1, 8)), -0.2, 0.2)), 0.1, 2.0)
    ocean_mask = touch_ends((jax.random.randint(keys[4], (NLAT, NLON), 0, 4) < 3).astype(jnp.int32), jax.random.fold_in(keys[4], 1), 0, 1)
    residual_rows = centred(keys[5], (ROW_W, ROWS), 1.0, 6.0, ((1, 32),), jnp.float32)
    dest_tile_keys = jax.random.split(jax.random.fold_in(keys[6], 1), ROWS // ROWS_DEV)
    dest_tile_turns = jax.random.permutation(jax.random.fold_in(keys[6], 3), ROWS // ROWS_DEV)
    dest_tile = jax.vmap(lambda own, number: deal_out(jax.random.fold_in(keys[6], 2), own, number, ROWS_DEV, N_LON, 1, CAP, 2))(dest_tile_keys, dest_tile_turns).reshape((ROWS, 1))
    dest_cell = touch_ends(jax.random.randint(keys[7], (ROWS,), 0, CLAT * CLON), jax.random.fold_in(keys[7], 1), 0, (CLAT * CLON) - 1).astype(jnp.int32)
    return dict(tide_state=tide_state, potential=potential, water_depth=water_depth, drag_coeff=drag_coeff, ocean_mask=ocean_mask, residual_rows=residual_rows, dest_tile=dest_tile, dest_cell=dest_cell)


OMEGAS = [1.405, 1.454, 1.379, 1.458, 0.729, 0.676, 0.725, 0.649]
RELAX_WEIGHT = 0.8


def divide(real_part, imag_part, diag, omega):
    denom = diag * diag + omega * omega
    return (real_part * diag + imag_part * omega) / denom, (imag_part * diag - real_part * omega) / denom


def update(center, potential, forcing, flux_lon, flux_lat, grad_lon, grad_lat, drag_coeff, coriolis, ocean, omega):
    eta_re, eta_im, east_re, east_im, north_re, north_im = center
    diag_vel = 1.0 + drag_coeff
    res_eta_re = (potential[0] - (eta_re - omega * eta_im + (flux_lon[0] + flux_lat[0]))) + forcing[0]
    res_eta_im = (potential[1] - (eta_im + omega * eta_re + (flux_lon[1] + flux_lat[1]))) + forcing[1]
    res_east_re = potential[2] - (diag_vel * east_re - omega * east_im - coriolis * north_re + grad_lon[0])
    res_east_im = potential[3] - (diag_vel * east_im + omega * east_re - coriolis * north_im + grad_lon[1])
    res_north_re = potential[4] - (diag_vel * north_re - omega * north_im + coriolis * east_re + grad_lat[0])
    res_north_im = potential[5] - (diag_vel * north_im + omega * north_re + coriolis * east_im + grad_lat[1])
    step_eta = divide(res_eta_re, res_eta_im, 1.0, omega)
    step_east = divide(res_east_re, res_east_im, diag_vel, omega)
    step_north = divide(res_north_re, res_north_im, diag_vel, omega)
    steps_all = (step_eta[0], step_eta[1], step_east[0], step_east[1], step_north[0], step_north[1])
    return tuple(ocean * (center[index] + RELAX_WEIGHT * steps_all[index]) for index in range(6))


def diff_lon(field):
    return (jnp.roll(field, -1, axis=1) - jnp.roll(field, 1, axis=1)) * 0.5


def diff_lat(field):
    zero_row = jnp.zeros_like(field[:1])
    upper = jnp.concatenate([field[1:], zero_row], axis=0)
    lower = jnp.concatenate([zero_row, field[:-1]], axis=0)
    return (upper - lower) * 0.5


def reference(tide_state, potential, water_depth, drag_coeff, ocean_mask, residual_rows, dest_tile, dest_cell):
    order = jnp.arange(ROWS, dtype=jnp.int32)
    lat_tile = order // (ROWS_DEV * N_LON)
    glob_lat = lat_tile * CLAT + dest_cell // CLON
    glob_lon = dest_tile[:, 0] * CLON + dest_cell % CLON
    flat_index = (glob_lat * NLON + glob_lon).astype(jnp.int32)
    forcing = jnp.zeros((ROW_W, NLAT * NLON), jnp.float32).at[:, flat_index].add(residual_rows)
    forcing = forcing.reshape(2, CONSTS, NLAT, NLON).transpose(1, 0, 2, 3)
    ocean = ocean_mask.astype(jnp.float32)
    lat_pos = (jnp.arange(NLAT).astype(jnp.float32) + 0.5) / NLAT - 0.5
    coriolis = (0.5 * jnp.sin(jnp.pi * lat_pos))[:, None]
    fields_all = tide_state.reshape(6, CONSTS, NLAT, NLON).transpose(1, 0, 2, 3)
    pot_all = potential.reshape(6, CONSTS, NLAT, NLON).transpose(1, 0, 2, 3)
    omegas = jnp.asarray(OMEGAS, jnp.float32)

    def single(items):
        fields, pot, force, omega = items
        center = tuple(fields[index] for index in range(6))
        for sweep_index in range(SWEEPS):
            flux_lon = (diff_lon(water_depth * center[2]), diff_lon(water_depth * center[3]))
            flux_lat = (diff_lat(water_depth * center[4]), diff_lat(water_depth * center[5]))
            grad_lon = (diff_lon(center[0]), diff_lon(center[1]))
            grad_lat = (diff_lat(center[0]), diff_lat(center[1]))
            center = update(center, pot, force, flux_lon, flux_lat, grad_lon, grad_lat, drag_coeff, coriolis, ocean, omega)
        return jnp.stack(center)

    result = lax.map(single, (fields_all, pot_all, forcing, omegas))
    return result.transpose(1, 0, 2, 3).reshape(FIELDS, NLAT, NLON)
```

```python
import functools

import jax
import jax.numpy as jnp
from jax import lax
from jax.experimental import pallas as pl
from jax.experimental.pallas import tpu as pltpu
from jax.sharding import PartitionSpec as P

OMEGAS = [1.405, 1.454, 1.379, 1.458, 0.729, 0.676, 0.725, 0.649]
RELAX = 0.8
LANES = 128
BLOCK = 256
HEAD = 8
MIB = 1 << 20
NT = (((1,), (1,)), ((), ()))
NN = (((1,), (0,)), ((), ()))
VMEM = pl.BlockSpec(memory_space=pltpu.VMEM)
SMEM = pl.BlockSpec(memory_space=pltpu.SMEM)


def iota(shape, dim):
    return lax.broadcasted_iota(jnp.int32, shape, dim)


def params(mib):
    return pltpu.CompilerParams(vmem_limit_bytes=mib * MIB)


def cost(flops, nbytes):
    return pl.CostEstimate(flops=flops, bytes_accessed=nbytes, transcendentals=0)


def rank_kernel(tiles, dest_ref, slot_ref, count_ref, base_ref, place_ref, total_ref):
    blocks, block = dest_ref.shape
    dest = dest_ref[...]
    upper = (iota((block, block), 0) < iota((block, block), 1)).astype(jnp.bfloat16)
    lane = iota((blocks, LANES), 1)
    slot = jnp.zeros((blocks, block), jnp.float32)
    base = jnp.zeros((blocks, 1), jnp.float32)
    counts = jnp.zeros((blocks, LANES), jnp.float32)
    bases = jnp.zeros((blocks, LANES), jnp.float32)
    for tile in range(tiles):
        mine = dest == tile
        ones = jnp.where(mine, 1.0, 0.0)
        before = lax.dot_general(
            ones.astype(jnp.bfloat16), upper, NN, preferred_element_type=jnp.float32
        )
        slot = slot + jnp.where(mine, before + base, 0.0)
        count = jnp.sum(ones, axis=1, keepdims=True)
        counts = counts + jnp.where(lane == tile, count, 0.0)
        bases = bases + jnp.where(lane == tile, base, 0.0)
        base = base + count
    lower = (iota((blocks, blocks), 1) < iota((blocks, blocks), 0)).astype(jnp.bfloat16)
    places = lax.dot_general(
        lower, counts.astype(jnp.bfloat16), NN, preferred_element_type=jnp.float32
    )
    slot_ref[...] = slot.astype(jnp.int32)
    count_ref[...] = counts.astype(jnp.int32)
    base_ref[...] = bases.astype(jnp.int32)
    place_ref[...] = places.astype(jnp.int32)
    total = jnp.sum(counts, axis=0, keepdims=True).astype(jnp.int32)
    total_ref[...] = jnp.broadcast_to(total, total_ref.shape)


def bucket_kernel(
    tiles, capacity, width, group, me_ref, count_ref, base_ref, place_ref, total_ref, *refs
):
    slot_ref, cell_ref, rows_ref = refs[:3]
    outs = refs[3 : 3 + tiles]
    staged, held = refs[3 + tiles :]
    blocks = slot_ref.shape[0]
    windows = capacity // LANES
    room = capacity + BLOCK
    chunk = max(8, 512 // tiles)
    row_of = iota((BLOCK, BLOCK), 0)
    third = iota((16, BLOCK), 0)
    pad = jnp.zeros((LANES - 2 * width - 16, BLOCK), jnp.bfloat16)

    def permute(at, first):
        block = first + at
        slot = slot_ref[pl.ds(block, 1), :]
        cell = cell_ref[pl.ds(block, 1), :]
        rows = rows_ref[:, pl.ds(pl.multiple_of(block * BLOCK, BLOCK), BLOCK)]
        high = rows.astype(jnp.bfloat16)
        low = (rows - high.astype(jnp.float32)).astype(jnp.bfloat16)
        cells = jnp.where(
            third == 0, cell >> 7, jnp.where(third == 1, cell & 127, 0)
        ).astype(jnp.float32)
        payload = jnp.concatenate([high, low, cells.astype(jnp.bfloat16), pad], axis=0)
        onehot = jnp.where(row_of == slot, 1.0, 0.0).astype(jnp.bfloat16)
        staged[pl.ds(pl.multiple_of(at * BLOCK, BLOCK), BLOCK), :] = lax.dot_general(
            onehot, payload, NT, preferred_element_type=jnp.float32
        )
        return first

    def spread(at, first):
        block = first + at
        for tile in range(tiles):
            count = count_ref[block, tile]
            source = at * BLOCK + base_ref[block, tile]
            place = tile * room + place_ref[block, tile]
            held[pl.ds(place, chunk), :] = staged[pl.ds(source, chunk), :]

            @pl.when(count > chunk)
            def _more():
                def step(part, carry):
                    held[pl.ds(place + part * chunk, chunk), :] = staged[
                        pl.ds(source + part * chunk, chunk), :
                    ]
                    return carry

                lax.fori_loop(1, pl.cdiv(count, chunk), step, 0)

        return first

    for part in range(blocks // group):
        lax.fori_loop(0, group, permute, part * group, unroll=2)
        lax.fori_loop(0, group, spread, part * group)

    row, lane = iota((32, LANES), 0), iota((32, LANES), 1)
    joined = jnp.where((row < width) & ((lane == row) | (lane == row + width)), 1.0, 0.0)
    joined = joined + jnp.where((row == width) & (lane == 2 * width), 128.0, 0.0)
    joined = joined + jnp.where((row == width) & (lane == 2 * width + 1), 1.0, 0.0)
    joined = joined.astype(jnp.bfloat16)
    lanes = iota((1, BLOCK), 1)
    me = me_ref[0]
    for step in range(tiles):
        tile = me ^ step
        count = total_ref[0, tile]
        out = outs[step]

        def turn(part, carry, tile=tile, count=count, out=out):
            block = held[pl.ds(pl.multiple_of(tile * room + part * BLOCK, 8), BLOCK), :]
            both = lax.dot_general(
                joined, block.astype(jnp.bfloat16), NT, preferred_element_type=jnp.float32
            )
            cells = jnp.where(lanes + part * BLOCK < count, both[width : width + 1], -1.0)
            for side in range(BLOCK // LANES):
                at = part * (BLOCK // LANES) + side
                cut = slice(side * LANES, (side + 1) * LANES)
                out[pl.ds(pl.multiple_of(at * width, width), width), :] = both[:width, cut]
                out[pl.ds(windows * width + at, 1), :] = cells[:, cut]
            return carry

        lax.fori_loop(0, pl.cdiv(count, BLOCK), turn, 0)
        out[windows * (width + 1) :, :] = jnp.full((HEAD, LANES), count, jnp.int32).astype(
            jnp.float32
        )


def sum_kernel(width, windows, amount, fresh, *refs):
    buckets = refs[:amount]
    out = refs[-1]
    half, wide = out.shape[1:]
    chunk = 2 * LANES
    if fresh:
        out[...] = jnp.zeros_like(out)
    else:
        out[...] = refs[amount][...]
    row_of = iota((half, chunk), 0)
    col_of = iota((wide, chunk), 0)
    for bucket in buckets:
        count = jnp.max(bucket[windows * (width + 1) :, :]).astype(jnp.int32)

        def step(part, carry, bucket=bucket):
            vals, cells = [], []
            for side in range(chunk // LANES):
                at = part * (chunk // LANES) + side
                vals.append(bucket[pl.ds(pl.multiple_of(at * width, width), width), :])
                cells.append(bucket[pl.ds(windows * width + at, 1), :])
            rows = jnp.concatenate(vals, axis=1)
            cell = jnp.concatenate(cells, axis=1).astype(jnp.int32)
            grid_row = cell >> 7
            low_row = jnp.where(cell < 0, -1, grid_row & (half - 1))
            column = (cell & 127) + jnp.where(grid_row >= half, LANES, 0)
            high = rows.astype(jnp.bfloat16)
            low = (rows - high.astype(jnp.float32)).astype(jnp.bfloat16)
            mine = row_of == low_row
            onehot = jnp.where(col_of == column, 1.0, 0.0).astype(jnp.bfloat16)
            left = []
            for channel in range(width):
                left.append(
                    jnp.concatenate(
                        [
                            jnp.where(mine, high[channel : channel + 1].astype(jnp.float32), 0.0),
                            jnp.where(mine, low[channel : channel + 1].astype(jnp.float32), 0.0),
                        ],
                        axis=1,
                    ).astype(jnp.bfloat16)
                )
            product = lax.dot_general(
                jnp.concatenate(left, axis=0),
                jnp.concatenate([onehot, onehot], axis=1),
                NT,
                preferred_element_type=jnp.float32,
            )
            out[...] += product.reshape(out.shape)
            return carry

        lax.fori_loop(0, pl.cdiv(count, chunk), step, 0)


def put_edges(strips, k, rows, r0, last_row, fields):
    north, south, west, east = strips
    eta_re, eta_im, east_re, east_im, north_re, north_im = fields
    lane = iota((rows, LANES), 1)
    part = pl.ds(r0, rows)
    for group, field in enumerate((eta_re, eta_im, east_re, east_im)):
        at = group * 8 + k
        west[part, :] = jnp.where(lane == at, pltpu.roll(field, at, 1), west[part, :])
        east[part, :] = jnp.where(lane == at, pltpu.roll(field, at + 1, 1), east[part, :])
    for group, field in enumerate((eta_re, eta_im, north_re, north_im)):
        at = group * 8 + k
        if r0 == 0:
            north[pl.ds(at, 1), :] = field[0:1]
        if r0 + rows == last_row:
            south[pl.ds(at, 1), :] = field[rows - 1 : rows]


def edges_kernel(rows, state_ref, depth_ref, *strips):
    k = pl.program_id(0)
    height = depth_ref.shape[0]
    for r0 in range(0, height, rows):
        part = slice(r0, r0 + rows)
        depth = depth_ref[part, :]
        fields = [state_ref[g, 0, part, :] for g in range(6)]
        fields = fields[:2] + [depth * field for field in fields[2:]]
        put_edges(strips, k, rows, r0, height, fields)


def force(force_ref, channel, r0, rows, half):
    side = r0 // half
    at = r0 % half
    return force_ref[channel, at : at + rows, side * LANES : (side + 1) * LANES]


def join_kernel(rows, omega_ref, eta_ref, east_ref, north_ref, depth_ref, ocean_ref, re_ref, im_ref, out_ref, *strips):
    k = pl.program_id(0)
    omega = omega_ref[k]
    weight = RELAX / (1.0 + omega * omega)
    height = depth_ref.shape[0]
    for r0 in range(0, height, rows):
        part = slice(r0, r0 + rows)
        depth = depth_ref[part, :]
        ocean = ocean_ref[part, :].astype(jnp.float32) * weight
        f_re = force(re_ref, 0, r0, rows, height // 2)
        f_im = force(im_ref, 0, r0, rows, height // 2)
        eta_re = eta_ref[0, 0, part, :] + ocean * (f_re + f_im * omega)
        eta_im = eta_ref[1, 0, part, :] + ocean * (f_im - f_re * omega)
        out_ref[0, 0, part, :] = eta_re
        out_ref[1, 0, part, :] = eta_im
        fields = [eta_re, eta_im] + [
            depth * ref[g, 0, part, :] for ref in (east_ref, north_ref) for g in range(2)
        ]
        put_edges(strips, k, rows, r0, height, fields)


def sweep_kernel(rows, forced, edges, *refs):
    refs = list(refs)
    omega_ref, eta_ref, vel_e_ref, vel_n_ref, pot_ref = refs[:5]
    depth_ref, drag_ref, ocean_ref, turn_ref = refs[5:9]
    north_in, south_in, west_in, east_in = refs[9:13]
    refs = refs[13:]
    if forced:
        re_ref, im_ref = refs[:2]
        refs = refs[2:]
    out_ref = refs[0]
    strips = refs[1:]
    k = pl.program_id(0)
    omega = omega_ref[k]
    inv_eta = 1.0 / (1.0 + omega * omega)
    height = depth_ref.shape[0]
    lane = iota((rows, LANES), 1)
    row = iota((rows, LANES), 0)

    def dlon(q, group, r0):
        at = group * 8 + k
        part = slice(r0, r0 + rows)
        left = pltpu.roll(q, 1, 1)
        right = pltpu.roll(q, LANES - 1, 1)
        w = pltpu.roll(west_in[part, :], (LANES - at) % LANES, 1)
        e = pltpu.roll(east_in[part, :], LANES - 1 - at, 1)
        return (jnp.where(lane == LANES - 1, e, right) - jnp.where(lane == 0, w, left)) * 0.5

    def shifted(q, first, last, group, r0):
        at = group * 8 + k
        above = first if r0 > 0 else north_in[pl.ds(at, 1), :]
        below = last if r0 + rows < height else south_in[pl.ds(at, 1), :]
        up = jnp.where(row == 0, above, pltpu.roll(q, 1, 0))
        down = jnp.where(row == rows - 1, below, pltpu.roll(q, rows - 1, 0))
        return (down - up) * 0.5

    for r0 in range(0, height, rows):
        part = slice(r0, r0 + rows)
        before = slice(max(r0 - 1, 0), max(r0 - 1, 0) + 1)
        after = slice(min(r0 + rows, height - 1), min(r0 + rows, height - 1) + 1)
        depth = depth_ref[part, :]
        diag = 1.0 + drag_ref[part, :]
        ocean = ocean_ref[part, :].astype(jnp.float32)
        turn = turn_ref[part, :]
        inv = 1.0 / (diag * diag + omega * omega)
        eta = [eta_ref[g, 0, part, :] for g in range(2)]
        east = [vel_e_ref[g, 0, part, :] for g in range(2)]
        north = [vel_n_ref[g, 0, part, :] for g in range(2)]
        pot = [pot_ref[g, 0, part, :] for g in range(6)]
        flux = []
        grad_lat = []
        for g in range(2):
            hn = depth * north[g]
            hn_first = depth_ref[before, :] * vel_n_ref[g, 0, before, :]
            hn_last = depth_ref[after, :] * vel_n_ref[g, 0, after, :]
            flux.append(
                dlon(depth * east[g], 2 + g, r0) + shifted(hn, hn_first, hn_last, 2 + g, r0)
            )
            grad_lat.append(
                shifted(eta[g], eta_ref[g, 0, before, :], eta_ref[g, 0, after, :], g, r0)
            )
        grad_lon = [dlon(eta[g], g, r0) for g in range(2)]
        res_re = pot[0] - (eta[0] - omega * eta[1] + flux[0])
        res_im = pot[1] - (eta[1] + omega * eta[0] + flux[1])
        if forced:
            res_re = res_re + force(re_ref, 0, r0, rows, height // 2)
            res_im = res_im + force(im_ref, 0, r0, rows, height // 2)
        weight = ocean * RELAX
        new = [
            ocean * eta[0] + weight * ((res_re + res_im * omega) * inv_eta),
            ocean * eta[1] + weight * ((res_im - res_re * omega) * inv_eta),
        ]
        scaled = weight * inv
        for own, other, grad, at, sign in (
            (east, north, grad_lon, 2, -1.0),
            (north, east, grad_lat, 4, 1.0),
        ):
            spun = [sign * (turn * other[g]) for g in range(2)]
            res_re = pot[at] - (diag * own[0] - omega * own[1] + spun[0] + grad[0])
            res_im = pot[at + 1] - (diag * own[1] + omega * own[0] + spun[1] + grad[1])
            new.append(ocean * own[0] + scaled * (res_re * diag + res_im * omega))
            new.append(ocean * own[1] + scaled * (res_im * diag - res_re * omega))
        for g in range(6):
            out_ref[g, 0, part, :] = new[g]
        if edges:
            put_edges(strips, k, rows, r0, height, new[:2] + [depth * q for q in new[2:]])


def local(
    tide_state, potential, water_depth, drag_coeff, ocean_mask, residual_rows, dest_tile, dest_cell
):
    f32 = jnp.float32
    tiles = lax.axis_size("lon")
    lats = lax.axis_size("lat")
    width, row_count = residual_rows.shape
    capacity = 2 * row_count // tiles
    height, across = water_depth.shape
    consts = tide_state.shape[0] // 6
    blocks = row_count // BLOCK
    windows = capacity // LANES
    bucket_rows = windows * (width + 1) + HEAD
    me = lax.axis_index("lon").reshape(1)

    omega = jnp.asarray(OMEGAS, f32)
    row_ids = lax.axis_index("lat") * height + jnp.arange(height, dtype=jnp.int32)
    lat_pos = (row_ids.astype(f32) + 0.5) / (height * lats) - 0.5
    turn = jnp.broadcast_to((0.5 * jnp.sin(jnp.pi * lat_pos))[:, None], (height, across))

    state = tide_state.reshape(6, consts, height, across)
    pot = potential.reshape(6, consts, height, across)
    chunk_rows = 32

    def fields(count, first):
        return pl.BlockSpec((count, 1, height, across), lambda k: (first // count, k, 0, 0))

    plane = pl.BlockSpec((height, across), lambda k: (0, 0))
    flat = pl.BlockSpec((4 * consts, across), lambda k: (0, 0))
    half_re = pl.BlockSpec((1, height // 2, 2 * across), lambda k: (k, 0, 0))
    half_im = pl.BlockSpec((1, height // 2, 2 * across), lambda k: (consts + k, 0, 0))
    strip_specs = [flat, flat, plane, plane]
    strip_shapes = [jax.ShapeDtypeStruct((4 * consts, across), f32)] * 2 + [
        jax.ShapeDtypeStruct((height, across), f32)
    ] * 2
    state_shape = jax.ShapeDtypeStruct(state.shape, f32)

    def exchange(strips):
        north, south, west, east = strips
        return (
            lax.ppermute(south, "lat", [(i, i + 1) for i in range(lats - 1)]),
            lax.ppermute(north, "lat", [(i + 1, i) for i in range(lats - 1)]),
            lax.ppermute(east, "lon", [(i, (i + 1) % tiles) for i in range(tiles)]),
            lax.ppermute(west, "lon", [((i + 1) % tiles, i) for i in range(tiles)]),
        )

    def sweep(eta, vel, strips, forcing, edges):
        forced = forcing is not None
        out = pl.pallas_call(
            functools.partial(sweep_kernel, chunk_rows, forced, edges),
            grid=(consts,),
            in_specs=[SMEM, fields(2, 0), fields(2, 2), fields(2, 4), fields(6, 0)]
            + [plane] * 4
            + strip_specs
            + ([half_re, half_im] if forced else []),
            out_specs=[fields(6, 0)] + (strip_specs if edges else []),
            out_shape=[state_shape] + (strip_shapes if edges else []),
            compiler_params=params(32),
            cost_estimate=cost(16 * 10**6, 9 * 10**6),
        )(
            omega, eta, vel, vel, pot, water_depth, drag_coeff, ocean_mask, turn, *strips,
            *((forcing, forcing) if forced else ()),
        )
        return out[0], out[1:]

    table = jax.ShapeDtypeStruct((blocks, LANES), jnp.int32)
    slot, counts, bases, places, totals = pl.pallas_call(
        functools.partial(rank_kernel, tiles),
        in_specs=[VMEM],
        out_specs=[VMEM] * 5,
        out_shape=[jax.ShapeDtypeStruct((blocks, BLOCK), jnp.int32), table, table, table]
        + [jax.ShapeDtypeStruct((8, LANES), jnp.int32)],
        compiler_params=params(32),
    )(dest_tile.reshape(blocks, BLOCK))

    strips = pl.pallas_call(
        functools.partial(edges_kernel, chunk_rows),
        grid=(consts,),
        in_specs=[fields(6, 0), plane],
        out_specs=strip_specs,
        out_shape=strip_shapes,
        compiler_params=params(32),
        cost_estimate=cost(10**6, 3 * 10**6),
    )(state, water_depth)
    strips = exchange(strips)

    group = min(32, blocks)
    buckets = pl.pallas_call(
        functools.partial(bucket_kernel, tiles, capacity, width, group),
        in_specs=[SMEM] * 5 + [VMEM] * 3,
        out_specs=[VMEM] * tiles,
        out_shape=[jax.ShapeDtypeStruct((bucket_rows, LANES), f32)] * tiles,
        scratch_shapes=[
            pltpu.VMEM(((group + 1) * BLOCK, LANES), f32),
            pltpu.VMEM((tiles * (capacity + BLOCK), LANES), f32),
        ],
        compiler_params=params(58),
        cost_estimate=cost(10**10, 7 * 10**6),
    )(me, counts, bases, places, totals, slot, dest_cell.reshape(blocks, BLOCK), residual_rows)

    grid_shape = jax.ShapeDtypeStruct((width, height // 2, 2 * across), f32)

    def add(parts, total):
        return pl.pallas_call(
            functools.partial(sum_kernel, width, windows, len(parts), total is None),
            in_specs=[VMEM] * (len(parts) + (total is not None)),
            out_specs=VMEM,
            out_shape=grid_shape,
            compiler_params=params(40),
            cost_estimate=cost(10**10, 3 * 10**6),
        )(*parts, *(() if total is None else (total,)))

    order = list(range(tiles // 2, tiles)) + list(range(1, tiles // 2))
    arrived = [
        lax.ppermute(buckets[s], "lon", [(i, i ^ s) for i in range(tiles)]) for s in order
    ]
    state, _ = sweep(state, state, strips, None, False)
    forcing = add([buckets[0]], None)
    each = tiles // 8
    for first in range(0, len(arrived), each):
        forcing = add(arrived[first : first + each], forcing)

    eta, *strips = pl.pallas_call(
        functools.partial(join_kernel, chunk_rows),
        grid=(consts,),
        in_specs=[
            SMEM,
            fields(2, 0),
            fields(2, 2),
            fields(2, 4),
            plane,
            plane,
            half_re,
            half_im,
        ],
        out_specs=[fields(2, 0)] + strip_specs,
        out_shape=[jax.ShapeDtypeStruct((2,) + state.shape[1:], f32)] + strip_shapes,
        compiler_params=params(32),
        cost_estimate=cost(10**6, 6 * 10**6),
    )(omega, state, state, state, water_depth, ocean_mask, forcing, forcing)
    state, strips = sweep(eta, state, exchange(strips), forcing, True)
    state, _ = sweep(state, state, exchange(strips), forcing, False)
    return state.reshape(tide_state.shape)


def solution(mesh):
    placed = (
        P(None, "lat", "lon"),
        P(None, "lat", "lon"),
        P("lat", "lon"),
        P("lat", "lon"),
        P("lat", "lon"),
        P(None, ("lat", "lon")),
        P(("lat", "lon"), None),
        P(("lat", "lon")),
    )
    return jax.shard_map(
        local, mesh=mesh, in_specs=placed, out_specs=P(None, "lat", "lon"), check_vma=False
    )
```

```python
import functools

import jax
import jax.numpy as jnp
from jax import lax
from jax.experimental import pallas as pl
from jax.experimental.pallas import tpu as pltpu
from jax.sharding import PartitionSpec as P

OMEGAS = [1.405, 1.454, 1.379, 1.458, 0.729, 0.676, 0.725, 0.649]
RELAX = 0.8
LANES = 128
BLOCK = 256
SPAN = 1024
SUM_SPAN = 1024
CUT_BITS = 11
HEAD = 8
MIB = 1 << 20
NT = (((1,), (1,)), ((), ()))
NN = (((1,), (0,)), ((), ()))
VMEM = pl.BlockSpec(memory_space=pltpu.VMEM)
SMEM = pl.BlockSpec(memory_space=pltpu.SMEM)


def iota(shape, dim):
    return lax.broadcasted_iota(jnp.int32, shape, dim)


def params(mib):
    return pltpu.CompilerParams(vmem_limit_bytes=mib * MIB)


def cost(flops, nbytes):
    return pl.CostEstimate(flops=flops, bytes_accessed=nbytes, transcendentals=0)


def rank_kernel(tiles, cuts, dest_ref, cell_ref, *outs):
    slot_ref, count_ref, base_ref, place_ref, total_ref = outs
    blocks, block = dest_ref.shape
    keys = dest_ref[...] * cuts + ((cell_ref[...] >> CUT_BITS) & (cuts - 1))
    upper = (iota((block, block), 0) < iota((block, block), 1)).astype(jnp.bfloat16)
    lane = iota((blocks, LANES), 1)
    slot = jnp.zeros((blocks, block), jnp.float32)
    base = jnp.zeros((blocks, 1), jnp.float32)
    counts = jnp.zeros((blocks, LANES), jnp.float32)
    bases = jnp.zeros((blocks, LANES), jnp.float32)
    for key in range(tiles * cuts):
        mine = keys == key
        ones = jnp.where(mine, 1.0, 0.0)
        before = lax.dot_general(
            ones.astype(jnp.bfloat16), upper, NN, preferred_element_type=jnp.float32
        )
        slot = slot + jnp.where(mine, before + base, 0.0)
        count = jnp.sum(ones, axis=1, keepdims=True)
        counts = jnp.where(lane == key, count, counts)
        bases = jnp.where(lane == key, base, bases)
        base = base + count
    lower = (iota((blocks, blocks), 1) < iota((blocks, blocks), 0)).astype(jnp.bfloat16)
    places = lax.dot_general(
        lower, counts.astype(jnp.bfloat16), NN, preferred_element_type=jnp.float32
    )
    total = jnp.broadcast_to(jnp.sum(counts, axis=0, keepdims=True), (8, LANES))
    first = jnp.zeros((8, LANES), jnp.float32)
    for back in range(1, cuts):
        inside = (iota((8, LANES), 1) & (cuts - 1)) >= back
        first = first + jnp.where(inside, pltpu.roll(total, back, 1), 0.0)
    most = jnp.max(counts, axis=1, keepdims=True)
    slot_ref[...] = slot.astype(jnp.int32)
    count_ref[...] = jnp.where(lane == LANES - 1, most, counts).astype(jnp.int32)
    base_ref[...] = bases.astype(jnp.int32)
    place_ref[...] = (places + first[0:1]).astype(jnp.int32)
    total_ref[...] = total.astype(jnp.int32)


def bucket_kernel(
    tiles, cuts, capacity, width, group, me_ref, count_ref, base_ref, place_ref, total_ref, *refs
):
    slot_ref, cell_ref, rows_ref = refs[:3]
    outs = refs[3 : 3 + tiles]
    staged, held = refs[3 + tiles :]
    blocks = slot_ref.shape[0]
    windows = capacity // LANES
    room = capacity + BLOCK
    chunk = 32
    inside = iota((chunk, LANES), 0)
    row_of = iota((BLOCK, BLOCK), 0)
    third = iota((16, BLOCK), 0)
    pad = jnp.zeros((LANES - 2 * width - 16, BLOCK), jnp.bfloat16)

    def permute(at, first):
        block = first + at
        slot = slot_ref[pl.ds(block, 1), :]
        cell = cell_ref[pl.ds(block, 1), :]
        rows = rows_ref[:, pl.ds(pl.multiple_of(block * BLOCK, BLOCK), BLOCK)]
        high = rows.astype(jnp.bfloat16)
        low = (rows - high.astype(jnp.float32)).astype(jnp.bfloat16)
        cells = jnp.where(
            third == 0, cell >> 7, jnp.where(third == 1, cell & 127, 0)
        ).astype(jnp.float32)
        payload = jnp.concatenate([high, low, cells.astype(jnp.bfloat16), pad], axis=0)
        onehot = jnp.where(row_of == slot, 1.0, 0.0).astype(jnp.bfloat16)
        staged[pl.ds(pl.multiple_of(at * BLOCK, BLOCK), BLOCK), :] = lax.dot_general(
            onehot, payload, NT, preferred_element_type=jnp.float32
        )
        return first

    def spread(at, first):
        block = first + at

        def move(key, part):
            count = count_ref[block, key]
            source = at * BLOCK + base_ref[block, key] + part * chunk
            place = (key // cuts) * room + place_ref[block, key] + part * chunk
            pltpu.store(
                held.at[pl.ds(place, chunk), :],
                staged[pl.ds(source, chunk), :],
                mask=inside < count - part * chunk,
            )

        for key in range(tiles * cuts):
            move(key, 0)

        @pl.when(count_ref[block, LANES - 1] > chunk)
        def _more():
            for key in range(tiles * cuts):

                def step(part, carry, key=key):
                    move(key, part)
                    return carry

                lax.fori_loop(1, pl.cdiv(count_ref[block, key], chunk), step, 0)

        return first

    for part in range(blocks // group):
        lax.fori_loop(0, group, permute, part * group, unroll=16)
        lax.fori_loop(0, group, spread, part * group)

    row, lane = iota((32, LANES), 0), iota((32, LANES), 1)
    joined = jnp.where((row < width) & ((lane == row) | (lane == row + width)), 1.0, 0.0)
    joined = joined + jnp.where((row == width) & (lane == 2 * width), 128.0, 0.0)
    joined = joined + jnp.where((row == width) & (lane == 2 * width + 1), 1.0, 0.0)
    joined = joined.astype(jnp.bfloat16)
    lanes = iota((1, BLOCK), 1)
    me = me_ref[0]
    for step in range(tiles):
        tile = me ^ step
        sizes = [total_ref[0, tile * cuts + cut] for cut in range(cuts)]
        count = functools.reduce(lambda a, b: a + b, sizes)
        out = outs[step]

        def turn(part, carry, tile=tile, count=count, out=out):
            for piece in range(SPAN // BLOCK):
                first = part * SPAN + piece * BLOCK
                block = held[pl.ds(pl.multiple_of(tile * room + first, 8), BLOCK), :]
                both = lax.dot_general(
                    joined, block.astype(jnp.bfloat16), NT, preferred_element_type=jnp.float32
                )
                cells = jnp.where(lanes + first < count, both[width : width + 1], -1.0)
                for side in range(BLOCK // LANES):
                    at = part * (SPAN // LANES) + piece * (BLOCK // LANES) + side
                    cut = slice(side * LANES, (side + 1) * LANES)
                    out[pl.ds(pl.multiple_of(at * width, width), width), :] = both[:width, cut]
                    out[pl.ds(windows * width + at, 1), :] = cells[:, cut]
            return carry

        lax.fori_loop(0, pl.cdiv(count, SPAN), turn, 0)
        line = iota((HEAD, LANES), 0)
        head = jnp.zeros((HEAD, LANES), jnp.int32)
        for cut in range(cuts):
            head = jnp.where(line == cut, sizes[cut], head)
        out[windows * (width + 1) :, :] = head.astype(jnp.float32)


def sum_kernel(width, windows, amount, cuts, fresh, *refs):
    buckets = refs[:amount]
    out = refs[-1]
    half, wide = out.shape[1:]
    high_of = half // cuts
    chunk = SUM_SPAN
    if fresh:
        out[...] = jnp.zeros_like(out)
    else:
        out[...] = refs[amount][...]
    row_of = iota((high_of, chunk), 0)
    col_of = iota((wide, chunk), 0)
    lanes = iota((1, LANES), 1)
    for bucket in buckets:
        top = windows * (width + 1)
        sizes = [
            jnp.max(bucket[top + cut : top + cut + 1, :]).astype(jnp.int32) for cut in range(cuts)
        ]
        total = functools.reduce(lambda a, b: a + b, sizes)
        start = jnp.int32(0)
        for cut in range(cuts):
            first = start // LANES
            start = start + sizes[cut]

            def step(part, carry, bucket=bucket, cut=cut, first=first):
                vals, cells = [], []
                for side in range(chunk // LANES):
                    at = first + part * (chunk // LANES) + side
                    read = jnp.minimum(at, windows - 1)
                    vals.append(bucket[pl.ds(pl.multiple_of(read * width, width), width), :])
                    cell = bucket[pl.ds(windows * width + read, 1), :]
                    cells.append(jnp.where(at * LANES + lanes < total, cell, -1.0))
                rows = jnp.concatenate(vals, axis=1)
                cell = jnp.concatenate(cells, axis=1).astype(jnp.int32)
                grid_row = cell >> 7
                low_row = jnp.where(cell < 0, -1, (grid_row & (half - 1)) - cut * high_of)
                column = (cell & 127) + jnp.where(grid_row >= half, LANES, 0)
                high = rows.astype(jnp.bfloat16)
                low = (rows - high.astype(jnp.float32)).astype(jnp.bfloat16)
                mine = row_of == low_row
                onehot = jnp.where(col_of == column, 1.0, 0.0).astype(jnp.bfloat16)
                left = []
                for channel in range(width):
                    one = slice(channel, channel + 1)
                    left.append(
                        jnp.concatenate(
                            [
                                jnp.where(mine, high[one].astype(jnp.float32), 0.0),
                                jnp.where(mine, low[one].astype(jnp.float32), 0.0),
                            ],
                            axis=1,
                        ).astype(jnp.bfloat16)
                    )
                product = lax.dot_general(
                    jnp.concatenate(left, axis=0),
                    jnp.concatenate([onehot, onehot], axis=1),
                    NT,
                    preferred_element_type=jnp.float32,
                )
                part_of = slice(cut * high_of, (cut + 1) * high_of)
                out[:, part_of, :] += product.reshape(width, high_of, wide)
                return carry

            lax.fori_loop(0, pl.cdiv(start - first * LANES, chunk), step, 0)


def put_edges(strips, k, rows, r0, last_row, fields):
    north, south, west, east = strips
    eta_re, eta_im, east_re, east_im, north_re, north_im = fields
    lane = iota((rows, LANES), 1)
    part = pl.ds(r0, rows)
    for group, field in enumerate((eta_re, eta_im, east_re, east_im)):
        at = group * 8 + k
        west[part, :] = jnp.where(lane == at, pltpu.roll(field, at, 1), west[part, :])
        east[part, :] = jnp.where(lane == at, pltpu.roll(field, at + 1, 1), east[part, :])
    for group, field in enumerate((eta_re, eta_im, north_re, north_im)):
        at = group * 8 + k
        if r0 == 0:
            north[pl.ds(at, 1), :] = field[0:1]
        if r0 + rows == last_row:
            south[pl.ds(at, 1), :] = field[rows - 1 : rows]


def edges_kernel(rows, state_ref, depth_ref, *strips):
    k = pl.program_id(0)
    height = depth_ref.shape[0]
    for r0 in range(0, height, rows):
        part = slice(r0, r0 + rows)
        depth = depth_ref[part, :]
        fields = [state_ref[g, 0, part, :] for g in range(6)]
        fields = fields[:2] + [depth * field for field in fields[2:]]
        put_edges(strips, k, rows, r0, height, fields)


def force(force_ref, channel, r0, rows, half):
    side = r0 // half
    at = r0 % half
    return force_ref[channel, at : at + rows, side * LANES : (side + 1) * LANES]


def join_kernel(rows, omega_ref, eta_ref, east_ref, north_ref, depth_ref, ocean_ref, re_ref, im_ref, out_ref, *strips):
    k = pl.program_id(0)
    omega = omega_ref[k]
    weight = RELAX / (1.0 + omega * omega)
    height = depth_ref.shape[0]
    for r0 in range(0, height, rows):
        part = slice(r0, r0 + rows)
        depth = depth_ref[part, :]
        ocean = ocean_ref[part, :].astype(jnp.float32) * weight
        f_re = force(re_ref, 0, r0, rows, height // 2)
        f_im = force(im_ref, 0, r0, rows, height // 2)
        eta_re = eta_ref[0, 0, part, :] + ocean * (f_re + f_im * omega)
        eta_im = eta_ref[1, 0, part, :] + ocean * (f_im - f_re * omega)
        out_ref[0, 0, part, :] = eta_re
        out_ref[1, 0, part, :] = eta_im
        fields = [eta_re, eta_im] + [
            depth * ref[g, 0, part, :] for ref in (east_ref, north_ref) for g in range(2)
        ]
        put_edges(strips, k, rows, r0, height, fields)


def sweep_kernel(rows, forced, edges, *refs):
    refs = list(refs)
    omega_ref, eta_ref, vel_e_ref, vel_n_ref, pot_ref = refs[:5]
    depth_ref, drag_ref, ocean_ref, turn_ref = refs[5:9]
    north_in, south_in, west_in, east_in = refs[9:13]
    refs = refs[13:]
    if forced:
        re_ref, im_ref = refs[:2]
        refs = refs[2:]
    out_ref = refs[0]
    strips = refs[1:]
    k = pl.program_id(0)
    omega = omega_ref[k]
    inv_eta = 1.0 / (1.0 + omega * omega)
    height = depth_ref.shape[0]
    lane = iota((rows, LANES), 1)
    row = iota((rows, LANES), 0)

    def dlon(q, group, r0):
        at = group * 8 + k
        part = slice(r0, r0 + rows)
        left = pltpu.roll(q, 1, 1)
        right = pltpu.roll(q, LANES - 1, 1)
        w = pltpu.roll(west_in[part, :], (LANES - at) % LANES, 1)
        e = pltpu.roll(east_in[part, :], LANES - 1 - at, 1)
        return (jnp.where(lane == LANES - 1, e, right) - jnp.where(lane == 0, w, left)) * 0.5

    def shifted(q, first, last, group, r0):
        at = group * 8 + k
        above = first if r0 > 0 else north_in[pl.ds(at, 1), :]
        below = last if r0 + rows < height else south_in[pl.ds(at, 1), :]
        up = jnp.where(row == 0, above, pltpu.roll(q, 1, 0))
        down = jnp.where(row == rows - 1, below, pltpu.roll(q, rows - 1, 0))
        return (down - up) * 0.5

    for r0 in range(0, height, rows):
        part = slice(r0, r0 + rows)
        before = slice(max(r0 - 1, 0), max(r0 - 1, 0) + 1)
        after = slice(min(r0 + rows, height - 1), min(r0 + rows, height - 1) + 1)
        depth = depth_ref[part, :]
        diag = 1.0 + drag_ref[part, :]
        ocean = ocean_ref[part, :].astype(jnp.float32)
        turn = turn_ref[part, :]
        inv = 1.0 / (diag * diag + omega * omega)
        eta = [eta_ref[g, 0, part, :] for g in range(2)]
        east = [vel_e_ref[g, 0, part, :] for g in range(2)]
        north = [vel_n_ref[g, 0, part, :] for g in range(2)]
        pot = [pot_ref[g, 0, part, :] for g in range(6)]
        flux = []
        grad_lat = []
        for g in range(2):
            hn = depth * north[g]
            hn_first = depth_ref[before, :] * vel_n_ref[g, 0, before, :]
            hn_last = depth_ref[after, :] * vel_n_ref[g, 0, after, :]
            flux.append(
                dlon(depth * east[g], 2 + g, r0) + shifted(hn, hn_first, hn_last, 2 + g, r0)
            )
            grad_lat.append(
                shifted(eta[g], eta_ref[g, 0, before, :], eta_ref[g, 0, after, :], g, r0)
            )
        grad_lon = [dlon(eta[g], g, r0) for g in range(2)]
        res_re = pot[0] - (eta[0] - omega * eta[1] + flux[0])
        res_im = pot[1] - (eta[1] + omega * eta[0] + flux[1])
        if forced:
            res_re = res_re + force(re_ref, 0, r0, rows, height // 2)
            res_im = res_im + force(im_ref, 0, r0, rows, height // 2)
        weight = ocean * RELAX
        new = [
            ocean * eta[0] + weight * ((res_re + res_im * omega) * inv_eta),
            ocean * eta[1] + weight * ((res_im - res_re * omega) * inv_eta),
        ]
        scaled = weight * inv
        for own, other, grad, at, sign in (
            (east, north, grad_lon, 2, -1.0),
            (north, east, grad_lat, 4, 1.0),
        ):
            spun = [sign * (turn * other[g]) for g in range(2)]
            res_re = pot[at] - (diag * own[0] - omega * own[1] + spun[0] + grad[0])
            res_im = pot[at + 1] - (diag * own[1] + omega * own[0] + spun[1] + grad[1])
            new.append(ocean * own[0] + scaled * (res_re * diag + res_im * omega))
            new.append(ocean * own[1] + scaled * (res_im * diag - res_re * omega))
        for g in range(6):
            out_ref[g, 0, part, :] = new[g]
        if edges:
            put_edges(strips, k, rows, r0, height, new[:2] + [depth * q for q in new[2:]])


def local(
    tide_state, potential, water_depth, drag_coeff, ocean_mask, residual_rows, dest_tile, dest_cell
):
    f32 = jnp.float32
    tiles = lax.axis_size("lon")
    lats = lax.axis_size("lat")
    width, row_count = residual_rows.shape
    capacity = 2 * row_count // tiles
    height, across = water_depth.shape
    consts = tide_state.shape[0] // 6
    blocks = row_count // BLOCK
    windows = capacity // LANES
    cuts = max(1, min(4, 32 // tiles))
    cells = dest_cell.reshape(blocks, BLOCK)
    bucket_rows = windows * (width + 1) + HEAD
    me = lax.axis_index("lon").reshape(1)

    omega = jnp.asarray(OMEGAS, f32)
    row_ids = lax.axis_index("lat") * height + jnp.arange(height, dtype=jnp.int32)
    lat_pos = (row_ids.astype(f32) + 0.5) / (height * lats) - 0.5
    turn = jnp.broadcast_to((0.5 * jnp.sin(jnp.pi * lat_pos))[:, None], (height, across))

    state = tide_state.reshape(6, consts, height, across)
    pot = potential.reshape(6, consts, height, across)
    chunk_rows = 32

    def fields(count, first):
        return pl.BlockSpec((count, 1, height, across), lambda k: (first // count, k, 0, 0))

    plane = pl.BlockSpec((height, across), lambda k: (0, 0))
    flat = pl.BlockSpec((4 * consts, across), lambda k: (0, 0))
    half_re = pl.BlockSpec((1, height // 2, 2 * across), lambda k: (k, 0, 0))
    half_im = pl.BlockSpec((1, height // 2, 2 * across), lambda k: (consts + k, 0, 0))
    strip_specs = [flat, flat, plane, plane]
    strip_shapes = [jax.ShapeDtypeStruct((4 * consts, across), f32)] * 2 + [
        jax.ShapeDtypeStruct((height, across), f32)
    ] * 2
    state_shape = jax.ShapeDtypeStruct(state.shape, f32)

    def exchange(strips):
        north, south, west, east = strips
        return (
            lax.ppermute(south, "lat", [(i, i + 1) for i in range(lats - 1)]),
            lax.ppermute(north, "lat", [(i + 1, i) for i in range(lats - 1)]),
            lax.ppermute(east, "lon", [(i, (i + 1) % tiles) for i in range(tiles)]),
            lax.ppermute(west, "lon", [((i + 1) % tiles, i) for i in range(tiles)]),
        )

    def sweep(eta, vel, strips, forcing, edges):
        forced = forcing is not None
        out = pl.pallas_call(
            functools.partial(sweep_kernel, chunk_rows, forced, edges),
            grid=(consts,),
            in_specs=[SMEM, fields(2, 0), fields(2, 2), fields(2, 4), fields(6, 0)]
            + [plane] * 4
            + strip_specs
            + ([half_re, half_im] if forced else []),
            out_specs=[fields(6, 0)] + (strip_specs if edges else []),
            out_shape=[state_shape] + (strip_shapes if edges else []),
            compiler_params=params(32),
            cost_estimate=cost(16 * 10**6, 9 * 10**6),
        )(
            omega, eta, vel, vel, pot, water_depth, drag_coeff, ocean_mask, turn, *strips,
            *((forcing, forcing) if forced else ()),
        )
        return out[0], out[1:]

    table = jax.ShapeDtypeStruct((blocks, LANES), jnp.int32)
    slot, counts, bases, places, totals = pl.pallas_call(
        functools.partial(rank_kernel, tiles, cuts),
        in_specs=[VMEM, VMEM],
        out_specs=[VMEM] * 5,
        out_shape=[jax.ShapeDtypeStruct((blocks, BLOCK), jnp.int32), table, table, table]
        + [jax.ShapeDtypeStruct((8, LANES), jnp.int32)],
        compiler_params=params(32),
    )(dest_tile.reshape(blocks, BLOCK), cells)

    strips = pl.pallas_call(
        functools.partial(edges_kernel, chunk_rows),
        grid=(consts,),
        in_specs=[fields(6, 0), plane],
        out_specs=strip_specs,
        out_shape=strip_shapes,
        compiler_params=params(32),
        cost_estimate=cost(10**6, 3 * 10**6),
    )(state, water_depth)
    strips = exchange(strips)

    group = min(32, blocks)
    buckets = pl.pallas_call(
        functools.partial(bucket_kernel, tiles, cuts, capacity, width, group),
        in_specs=[SMEM] * 5 + [VMEM] * 3,
        out_specs=[VMEM] * tiles,
        out_shape=[jax.ShapeDtypeStruct((bucket_rows, LANES), f32)] * tiles,
        scratch_shapes=[
            pltpu.VMEM(((group + 1) * BLOCK, LANES), f32),
            pltpu.VMEM((tiles * (capacity + BLOCK), LANES), f32),
        ],
        compiler_params=params(58),
        cost_estimate=cost(10**10, 7 * 10**6),
    )(me, counts, bases, places, totals, slot, cells, residual_rows)

    grid_shape = jax.ShapeDtypeStruct((width, height // 2, 2 * across), f32)

    def add(parts, total):
        return pl.pallas_call(
            functools.partial(sum_kernel, width, windows, len(parts), cuts, total is None),
            in_specs=[VMEM] * (len(parts) + (total is not None)),
            out_specs=VMEM,
            out_shape=grid_shape,
            compiler_params=params(40),
            cost_estimate=cost(10**10, 3 * 10**6),
        )(*parts, *(() if total is None else (total,)))

    order = list(range(tiles // 2, tiles)) + list(range(1, tiles // 2))
    arrived = [
        lax.ppermute(buckets[s], "lon", [(i, i ^ s) for i in range(tiles)]) for s in order
    ]
    state, _ = sweep(state, state, strips, None, False)
    forcing = add([buckets[0]], None)
    each = tiles // 8
    for first in range(0, len(arrived), each):
        forcing = add(arrived[first : first + each], forcing)

    eta, *strips = pl.pallas_call(
        functools.partial(join_kernel, chunk_rows),
        grid=(consts,),
        in_specs=[
            SMEM,
            fields(2, 0),
            fields(2, 2),
            fields(2, 4),
            plane,
            plane,
            half_re,
            half_im,
        ],
        out_specs=[fields(2, 0)] + strip_specs,
        out_shape=[jax.ShapeDtypeStruct((2,) + state.shape[1:], f32)] + strip_shapes,
        compiler_params=params(32),
        cost_estimate=cost(10**6, 6 * 10**6),
    )(omega, state, state, state, water_depth, ocean_mask, forcing, forcing)
    state, strips = sweep(eta, state, exchange(strips), forcing, True)
    state, _ = sweep(state, state, exchange(strips), forcing, False)
    return state.reshape(tide_state.shape)


def solution(mesh):
    placed = (
        P(None, "lat", "lon"),
        P(None, "lat", "lon"),
        P("lat", "lon"),
        P("lat", "lon"),
        P("lat", "lon"),
        P(None, ("lat", "lon")),
        P(("lat", "lon"), None),
        P(("lat", "lon")),
    )
    return jax.shard_map(
        local, mesh=mesh, in_specs=placed, out_specs=P(None, "lat", "lon"), check_vma=False
    )
```

```python
import functools

import jax
import jax.numpy as jnp
from jax import lax
from jax.experimental import pallas as pl
from jax.experimental.pallas import tpu as pltpu
from jax.sharding import PartitionSpec as P

OMEGAS = [1.405, 1.454, 1.379, 1.458, 0.729, 0.676, 0.725, 0.649]
RELAX = 0.8
LANES = 128
BLOCK = 256
SPAN = 2048
SUM_SPAN = 1024
CUT_BITS = 11
HEAD = 8
MIB = 1 << 20
NT = (((1,), (1,)), ((), ()))
NN = (((1,), (0,)), ((), ()))
VMEM = pl.BlockSpec(memory_space=pltpu.VMEM)
SMEM = pl.BlockSpec(memory_space=pltpu.SMEM)
ANY = pl.BlockSpec(memory_space=pl.ANY)


def iota(shape, dim):
    return lax.broadcasted_iota(jnp.int32, shape, dim)


def params(mib):
    return pltpu.CompilerParams(vmem_limit_bytes=mib * MIB)


def cost(flops, nbytes):
    return pl.CostEstimate(flops=flops, bytes_accessed=nbytes, transcendentals=0)


def rank_kernel(tiles, cuts, dest_ref, cell_ref, *outs):
    slot_ref, table_ref = outs
    blocks, block = dest_ref.shape[0] // 2, BLOCK

    def lines(ref):
        return jnp.concatenate(
            [ref[pl.ds(side, blocks, stride=2), :] for side in range(2)], axis=1
        )

    tile = lines(dest_ref) ^ lax.axis_index("lon")
    keys = tile * cuts + ((lines(cell_ref) >> CUT_BITS) & (cuts - 1))
    upper = (iota((block, block), 0) < iota((block, block), 1)).astype(jnp.bfloat16)
    lane = iota((blocks, LANES), 1)
    slot = jnp.zeros((blocks, block), jnp.float32)
    base = jnp.zeros((blocks, 1), jnp.float32)
    counts = jnp.zeros((blocks, LANES), jnp.float32)
    bases = jnp.zeros((blocks, LANES), jnp.float32)
    for key in range(tiles * cuts):
        mine = keys == key
        ones = jnp.where(mine, 1.0, 0.0)
        before = lax.dot_general(
            ones.astype(jnp.bfloat16), upper, NN, preferred_element_type=jnp.float32
        )
        slot = slot + jnp.where(mine, before + base, 0.0)
        count = jnp.sum(ones, axis=1, keepdims=True)
        counts = jnp.where(lane == key, count, counts)
        bases = jnp.where(lane == key, base, bases)
        base = base + count
    lower = (iota((blocks, blocks), 1) < iota((blocks, blocks), 0)).astype(jnp.bfloat16)
    places = lax.dot_general(
        lower, counts.astype(jnp.bfloat16), NN, preferred_element_type=jnp.float32
    )
    total = jnp.broadcast_to(jnp.sum(counts, axis=0, keepdims=True), (8, LANES))
    first = jnp.zeros((8, LANES), jnp.float32)
    for back in range(1, cuts):
        inside = (iota((8, LANES), 1) & (cuts - 1)) >= back
        first = first + jnp.where(inside, pltpu.roll(total, back, 1), 0.0)
    most = jnp.max(counts, axis=1, keepdims=True)
    slot_ref[...] = slot.astype(jnp.int32)
    table_ref[:blocks, :] = jnp.where(lane == LANES - 1, most, counts).astype(jnp.int32)
    table_ref[blocks : 2 * blocks, :] = bases.astype(jnp.int32)
    table_ref[2 * blocks : 3 * blocks, :] = (places + first[0:1]).astype(jnp.int32)
    table_ref[3 * blocks :, :] = total.astype(jnp.int32)


def bucket_kernel(tiles, cuts, capacity, width, group, table_ref, *refs):
    slot_ref, cell_ref, rows_any = refs[:3]
    outs = refs[3 : 3 + tiles]
    staged, held, turned, rows_ref, read_sem, write_sem = refs[3 + tiles :]
    keys = tiles * cuts
    blocks = slot_ref.shape[0]
    windows = capacity // LANES
    room = capacity + BLOCK
    chunk = 32
    inside = iota((chunk, LANES), 0)
    row_of = iota((BLOCK, BLOCK), 0)
    third = iota((16, BLOCK), 0)
    pad = jnp.zeros((LANES - 2 * width - 16, BLOCK), jnp.bfloat16)

    def permute(at, first):
        block = first + at
        slot = slot_ref[pl.ds(block, 1), :]
        cell = jnp.concatenate(
            [cell_ref[pl.ds(2 * block + side, 1), :] for side in range(2)], axis=1
        )
        rows = rows_ref[:, pl.ds(pl.multiple_of(block * BLOCK, BLOCK), BLOCK)]
        high = rows.astype(jnp.bfloat16)
        low = (rows - high.astype(jnp.float32)).astype(jnp.bfloat16)
        cells = jnp.where(
            third == 0, cell >> 7, jnp.where(third == 1, cell & 127, 0)
        ).astype(jnp.float32)
        payload = jnp.concatenate([high, low, cells.astype(jnp.bfloat16), pad], axis=0)
        onehot = jnp.where(row_of == slot, 1.0, 0.0).astype(jnp.bfloat16)
        staged[pl.ds(pl.multiple_of(at * BLOCK, BLOCK), BLOCK), :] = lax.dot_general(
            onehot, payload, NT, preferred_element_type=jnp.float32
        )
        return first

    def move(at, block, key, part):
        count = table_ref[block, key]
        source = at * BLOCK + table_ref[blocks + block, key] + part * chunk
        place = (key // cuts) * room + table_ref[2 * blocks + block, key] + part * chunk
        pltpu.store(
            held.at[pl.ds(place, chunk), :],
            staged[pl.ds(source, chunk), :],
            mask=inside < count - part * chunk,
        )

    def spread(at, first):
        for key in range(keys):
            move(at, first + at, key, 0)
        return first

    def spread_rest(at, first):
        block = first + at

        @pl.when(table_ref[block, LANES - 1] > chunk)
        def _more():
            for key in range(keys):

                def step(part, carry, key=key):
                    move(at, block, key, part)
                    return carry

                lax.fori_loop(1, pl.cdiv(table_ref[block, key], chunk), step, 0)

        return first

    span = group * BLOCK
    reads = [
        pltpu.make_async_copy(
            rows_any.at[:, part * span : (part + 1) * span],
            rows_ref.at[:, part * span : (part + 1) * span],
            read_sem.at[part],
        )
        for part in range(blocks // group)
    ]
    for read in reads:
        read.start()
    for part in range(blocks // group):
        reads[part].wait()
        lax.fori_loop(0, group, permute, part * group, unroll=16)
        lax.fori_loop(0, group, spread, part * group, unroll=4)
        lax.fori_loop(0, group, spread_rest, part * group)

    row, lane = iota((32, LANES), 0), iota((32, LANES), 1)
    joined = jnp.where((row < width) & ((lane == row) | (lane == row + width)), 1.0, 0.0)
    joined = joined + jnp.where((row == width) & (lane == 2 * width), 128.0, 0.0)
    joined = joined + jnp.where((row == width) & (lane == 2 * width + 1), 1.0, 0.0)
    joined = joined.astype(jnp.bfloat16)
    lanes = iota((1, BLOCK), 1)
    writes = []
    for tile in range(tiles):
        out = turned.at[tile]
        sizes = [table_ref[3 * blocks, tile * cuts + cut] for cut in range(cuts)]
        count = functools.reduce(lambda a, b: a + b, sizes)

        def turn(part, carry, tile=tile, count=count, out=out):
            for piece in range(SPAN // BLOCK):
                first = part * SPAN + piece * BLOCK
                block = held[pl.ds(pl.multiple_of(tile * room + first, 8), BLOCK), :]
                both = lax.dot_general(
                    joined, block.astype(jnp.bfloat16), NT, preferred_element_type=jnp.float32
                )
                cells = jnp.where(lanes + first < count, both[width : width + 1], -1.0)
                for side in range(BLOCK // LANES):
                    at = part * (SPAN // LANES) + piece * (BLOCK // LANES) + side
                    cut = slice(side * LANES, (side + 1) * LANES)
                    out[pl.ds(pl.multiple_of(at * width, width), width), :] = both[:width, cut]
                    out[pl.ds(windows * width + at, 1), :] = cells[:, cut]
            return carry

        lax.fori_loop(0, pl.cdiv(count, SPAN), turn, 0)
        line = iota((HEAD, LANES), 0)
        head = jnp.zeros((HEAD, LANES), jnp.int32)
        for cut in range(cuts):
            head = jnp.where(line == cut, sizes[cut], head)
        out[windows * (width + 1) :, :] = head.astype(jnp.float32)
        writes.append(pltpu.make_async_copy(out, outs[tile], write_sem.at[tile]))
        writes[-1].start()
    for write in writes:
        write.wait()


def sum_kernel(width, windows, amount, cuts, fresh, *refs):
    buckets = refs[:amount]
    out = refs[-1]
    half, wide = out.shape[1:]
    high_of = half // cuts
    chunk = SUM_SPAN
    if fresh:
        out[...] = jnp.zeros_like(out)
    else:
        out[...] = refs[amount][...]
    row_of = iota((high_of, chunk), 0)
    col_of = iota((wide, chunk), 0)
    lanes = iota((1, LANES), 1)
    for bucket in buckets:
        top = windows * (width + 1)
        sizes = [
            jnp.max(bucket[top + cut : top + cut + 1, :]).astype(jnp.int32) for cut in range(cuts)
        ]
        total = functools.reduce(lambda a, b: a + b, sizes)
        start = jnp.int32(0)
        for cut in range(cuts):
            first = start // LANES
            start = start + sizes[cut]

            def step(part, carry, bucket=bucket, cut=cut, first=first):
                vals, cells = [], []
                for side in range(chunk // LANES):
                    at = first + part * (chunk // LANES) + side
                    read = jnp.minimum(at, windows - 1)
                    vals.append(bucket[pl.ds(pl.multiple_of(read * width, width), width), :])
                    cell = bucket[pl.ds(windows * width + read, 1), :]
                    cells.append(jnp.where(at * LANES + lanes < total, cell, -1.0))
                rows = jnp.concatenate(vals, axis=1)
                cell = jnp.concatenate(cells, axis=1).astype(jnp.int32)
                grid_row = cell >> 7
                low_row = jnp.where(cell < 0, -1, (grid_row & (half - 1)) - cut * high_of)
                column = (cell & 127) + jnp.where(grid_row >= half, LANES, 0)
                high = rows.astype(jnp.bfloat16)
                low = (rows - high.astype(jnp.float32)).astype(jnp.bfloat16)
                mine = row_of == low_row
                onehot = jnp.where(col_of == column, 1.0, 0.0).astype(jnp.bfloat16)
                left = []
                for channel in range(width):
                    one = slice(channel, channel + 1)
                    left.append(
                        jnp.concatenate(
                            [
                                jnp.where(mine, high[one].astype(jnp.float32), 0.0),
                                jnp.where(mine, low[one].astype(jnp.float32), 0.0),
                            ],
                            axis=1,
                        ).astype(jnp.bfloat16)
                    )
                product = lax.dot_general(
                    jnp.concatenate(left, axis=0),
                    jnp.concatenate([onehot, onehot], axis=1),
                    NT,
                    preferred_element_type=jnp.float32,
                )
                part_of = slice(cut * high_of, (cut + 1) * high_of)
                out[:, part_of, :] += product.reshape(width, high_of, wide)
                return carry

            lax.fori_loop(0, pl.cdiv(start - first * LANES, chunk), step, 0)


def put_edges(strips, k, rows, r0, last_row, fields):
    north, south, west, east = strips
    eta_re, eta_im, east_re, east_im, north_re, north_im = fields
    lane = iota((rows, LANES), 1)
    part = pl.ds(r0, rows)
    for group, field in enumerate((eta_re, eta_im, east_re, east_im)):
        at = group * 8 + k
        west[part, :] = jnp.where(lane == at, pltpu.roll(field, at, 1), west[part, :])
        east[part, :] = jnp.where(lane == at, pltpu.roll(field, at + 1, 1), east[part, :])
    for group, field in enumerate((eta_re, eta_im, north_re, north_im)):
        at = group * 8 + k
        if r0 == 0:
            north[pl.ds(at, 1), :] = field[0:1]
        if r0 + rows == last_row:
            south[pl.ds(at, 1), :] = field[rows - 1 : rows]


def edges_kernel(rows, state_ref, depth_ref, *strips):
    k = pl.program_id(0)
    height = depth_ref.shape[0]
    for r0 in range(0, height, rows):
        part = slice(r0, r0 + rows)
        depth = depth_ref[part, :]
        fields = [state_ref[g, 0, part, :] for g in range(6)]
        fields = fields[:2] + [depth * field for field in fields[2:]]
        put_edges(strips, k, rows, r0, height, fields)


def force(force_ref, channel, r0, rows, half):
    side = r0 // half
    at = r0 % half
    return force_ref[channel, at : at + rows, side * LANES : (side + 1) * LANES]


def join_kernel(rows, omega_ref, eta_ref, east_ref, north_ref, depth_ref, ocean_ref, re_ref, im_ref, out_ref, *strips):
    k = pl.program_id(0)
    omega = omega_ref[k]
    weight = RELAX / (1.0 + omega * omega)
    height = depth_ref.shape[0]
    for r0 in range(0, height, rows):
        part = slice(r0, r0 + rows)
        depth = depth_ref[part, :]
        ocean = ocean_ref[part, :].astype(jnp.float32) * weight
        f_re = force(re_ref, 0, r0, rows, height // 2)
        f_im = force(im_ref, 0, r0, rows, height // 2)
        eta_re = eta_ref[0, 0, part, :] + ocean * (f_re + f_im * omega)
        eta_im = eta_ref[1, 0, part, :] + ocean * (f_im - f_re * omega)
        out_ref[0, 0, part, :] = eta_re
        out_ref[1, 0, part, :] = eta_im
        fields = [eta_re, eta_im] + [
            depth * ref[g, 0, part, :] for ref in (east_ref, north_ref) for g in range(2)
        ]
        put_edges(strips, k, rows, r0, height, fields)


def sweep_kernel(rows, forced, edges, *refs):
    refs = list(refs)
    omega_ref, eta_ref, vel_e_ref, vel_n_ref, pot_ref = refs[:5]
    depth_ref, drag_ref, ocean_ref, turn_ref = refs[5:9]
    north_in, south_in, west_in, east_in = refs[9:13]
    refs = refs[13:]
    if forced:
        re_ref, im_ref = refs[:2]
        refs = refs[2:]
    out_ref = refs[0]
    strips = refs[1:]
    k = pl.program_id(0)
    omega = omega_ref[k]
    inv_eta = 1.0 / (1.0 + omega * omega)
    height = depth_ref.shape[0]
    lane = iota((rows, LANES), 1)
    row = iota((rows, LANES), 0)

    def dlon(q, group, r0):
        at = group * 8 + k
        part = slice(r0, r0 + rows)
        left = pltpu.roll(q, 1, 1)
        right = pltpu.roll(q, LANES - 1, 1)
        w = pltpu.roll(west_in[part, :], (LANES - at) % LANES, 1)
        e = pltpu.roll(east_in[part, :], LANES - 1 - at, 1)
        return (jnp.where(lane == LANES - 1, e, right) - jnp.where(lane == 0, w, left)) * 0.5

    def shifted(q, first, last, group, r0):
        at = group * 8 + k
        above = first if r0 > 0 else north_in[pl.ds(at, 1), :]
        below = last if r0 + rows < height else south_in[pl.ds(at, 1), :]
        up = jnp.where(row == 0, above, pltpu.roll(q, 1, 0))
        down = jnp.where(row == rows - 1, below, pltpu.roll(q, rows - 1, 0))
        return (down - up) * 0.5

    for r0 in range(0, height, rows):
        part = slice(r0, r0 + rows)
        before = slice(max(r0 - 1, 0), max(r0 - 1, 0) + 1)
        after = slice(min(r0 + rows, height - 1), min(r0 + rows, height - 1) + 1)
        depth = depth_ref[part, :]
        diag = 1.0 + drag_ref[part, :]
        ocean = ocean_ref[part, :].astype(jnp.float32)
        turn = turn_ref[part, :]
        inv = 1.0 / (diag * diag + omega * omega)
        eta = [eta_ref[g, 0, part, :] for g in range(2)]
        east = [vel_e_ref[g, 0, part, :] for g in range(2)]
        north = [vel_n_ref[g, 0, part, :] for g in range(2)]
        pot = [pot_ref[g, 0, part, :] for g in range(6)]
        flux = []
        grad_lat = []
        for g in range(2):
            hn = depth * north[g]
            hn_first = depth_ref[before, :] * vel_n_ref[g, 0, before, :]
            hn_last = depth_ref[after, :] * vel_n_ref[g, 0, after, :]
            flux.append(
                dlon(depth * east[g], 2 + g, r0) + shifted(hn, hn_first, hn_last, 2 + g, r0)
            )
            grad_lat.append(
                shifted(eta[g], eta_ref[g, 0, before, :], eta_ref[g, 0, after, :], g, r0)
            )
        grad_lon = [dlon(eta[g], g, r0) for g in range(2)]
        res_re = pot[0] - (eta[0] - omega * eta[1] + flux[0])
        res_im = pot[1] - (eta[1] + omega * eta[0] + flux[1])
        if forced:
            res_re = res_re + force(re_ref, 0, r0, rows, height // 2)
            res_im = res_im + force(im_ref, 0, r0, rows, height // 2)
        weight = ocean * RELAX
        new = [
            ocean * eta[0] + weight * ((res_re + res_im * omega) * inv_eta),
            ocean * eta[1] + weight * ((res_im - res_re * omega) * inv_eta),
        ]
        scaled = weight * inv
        for own, other, grad, at, sign in (
            (east, north, grad_lon, 2, -1.0),
            (north, east, grad_lat, 4, 1.0),
        ):
            spun = [sign * (turn * other[g]) for g in range(2)]
            res_re = pot[at] - (diag * own[0] - omega * own[1] + spun[0] + grad[0])
            res_im = pot[at + 1] - (diag * own[1] + omega * own[0] + spun[1] + grad[1])
            new.append(ocean * own[0] + scaled * (res_re * diag + res_im * omega))
            new.append(ocean * own[1] + scaled * (res_im * diag - res_re * omega))
        for g in range(6):
            out_ref[g, 0, part, :] = new[g]
        if edges:
            put_edges(strips, k, rows, r0, height, new[:2] + [depth * q for q in new[2:]])


def local(
    tide_state, potential, water_depth, drag_coeff, ocean_mask, residual_rows, dest_tile, dest_cell
):
    f32 = jnp.float32
    tiles = lax.axis_size("lon")
    lats = lax.axis_size("lat")
    width, row_count = residual_rows.shape
    capacity = 2 * row_count // tiles
    height, across = water_depth.shape
    consts = tide_state.shape[0] // 6
    blocks = row_count // BLOCK
    windows = capacity // LANES
    cuts = max(1, min(4, 32 // tiles))
    cells = dest_cell.reshape(2 * blocks, LANES)
    bucket_rows = windows * (width + 1) + HEAD

    omega = jnp.asarray(OMEGAS, f32)
    row_ids = lax.axis_index("lat") * height + jnp.arange(height, dtype=jnp.int32)
    lat_pos = (row_ids.astype(f32) + 0.5) / (height * lats) - 0.5
    turn = jnp.broadcast_to((0.5 * jnp.sin(jnp.pi * lat_pos))[:, None], (height, across))

    state = tide_state.reshape(6, consts, height, across)
    pot = potential.reshape(6, consts, height, across)
    chunk_rows = 32

    def fields(count, first):
        return pl.BlockSpec((count, 1, height, across), lambda k: (first // count, k, 0, 0))

    plane = pl.BlockSpec((height, across), lambda k: (0, 0))
    flat = pl.BlockSpec((4 * consts, across), lambda k: (0, 0))
    half_re = pl.BlockSpec((1, height // 2, 2 * across), lambda k: (k, 0, 0))
    half_im = pl.BlockSpec((1, height // 2, 2 * across), lambda k: (consts + k, 0, 0))
    strip_specs = [flat, flat, plane, plane]
    strip_shapes = [jax.ShapeDtypeStruct((4 * consts, across), f32)] * 2 + [
        jax.ShapeDtypeStruct((height, across), f32)
    ] * 2
    state_shape = jax.ShapeDtypeStruct(state.shape, f32)

    def exchange(strips):
        north, south, west, east = strips
        return (
            lax.ppermute(south, "lat", [(i, i + 1) for i in range(lats - 1)]),
            lax.ppermute(north, "lat", [(i + 1, i) for i in range(lats - 1)]),
            lax.ppermute(east, "lon", [(i, (i + 1) % tiles) for i in range(tiles)]),
            lax.ppermute(west, "lon", [((i + 1) % tiles, i) for i in range(tiles)]),
        )

    def sweep(eta, vel, strips, forcing, edges):
        forced = forcing is not None
        out = pl.pallas_call(
            functools.partial(sweep_kernel, chunk_rows, forced, edges),
            grid=(consts,),
            in_specs=[SMEM, fields(2, 0), fields(2, 2), fields(2, 4), fields(6, 0)]
            + [plane] * 4
            + strip_specs
            + ([half_re, half_im] if forced else []),
            out_specs=[fields(6, 0)] + (strip_specs if edges else []),
            out_shape=[state_shape] + (strip_shapes if edges else []),
            compiler_params=params(32),
            cost_estimate=cost(16 * 10**6, 9 * 10**6),
        )(
            omega, eta, vel, vel, pot, water_depth, drag_coeff, ocean_mask, turn, *strips,
            *((forcing, forcing) if forced else ()),
        )
        return out[0], out[1:]

    slot, table = pl.pallas_call(
        functools.partial(rank_kernel, tiles, cuts),
        in_specs=[VMEM, VMEM],
        out_specs=[VMEM] * 2,
        out_shape=[
            jax.ShapeDtypeStruct((blocks, BLOCK), jnp.int32),
            jax.ShapeDtypeStruct((3 * blocks + 8, LANES), jnp.int32),
        ],
        compiler_params=params(32),
    )(dest_tile.reshape(2 * blocks, LANES), cells)

    strips = pl.pallas_call(
        functools.partial(edges_kernel, chunk_rows),
        grid=(consts,),
        in_specs=[fields(6, 0), plane],
        out_specs=strip_specs,
        out_shape=strip_shapes,
        compiler_params=params(32),
        cost_estimate=cost(10**6, 3 * 10**6),
    )(state, water_depth)
    strips = exchange(strips)

    group = min(32, blocks)

    buckets = pl.pallas_call(
        functools.partial(bucket_kernel, tiles, cuts, capacity, width, group),
        in_specs=[SMEM, VMEM, VMEM, ANY],
        out_specs=[ANY] * tiles,
        out_shape=[jax.ShapeDtypeStruct((bucket_rows, LANES), f32)] * tiles,
        scratch_shapes=[
            pltpu.VMEM(((group + 1) * BLOCK, LANES), f32),
            pltpu.VMEM((tiles * (capacity + BLOCK), LANES), f32),
            pltpu.VMEM((tiles, bucket_rows, LANES), f32),
            pltpu.VMEM((width, row_count), f32),
            pltpu.SemaphoreType.DMA((blocks // group,)),
            pltpu.SemaphoreType.DMA((tiles,)),
        ],
        compiler_params=params(60),
        cost_estimate=cost(10**10, 7 * 10**6),
    )(table, slot, cells, residual_rows)

    grid_shape = jax.ShapeDtypeStruct((width, height // 2, 2 * across), f32)

    def add(parts, total):
        return pl.pallas_call(
            functools.partial(sum_kernel, width, windows, len(parts), cuts, total is None),
            in_specs=[VMEM] * (len(parts) + (total is not None)),
            out_specs=VMEM,
            out_shape=grid_shape,
            compiler_params=params(40),
            cost_estimate=cost(10**10, 3 * 10**6),
        )(*parts, *(() if total is None else (total,)))

    order = list(range(tiles // 2, tiles)) + list(range(1, tiles // 2))
    arrived = [
        lax.ppermute(buckets[s], "lon", [(i, i ^ s) for i in range(tiles)]) for s in order
    ]
    state, _ = sweep(state, state, strips, None, False)
    forcing = add([buckets[0]], None)
    each = tiles // 8
    for first in range(0, len(arrived), each):
        forcing = add(arrived[first : first + each], forcing)

    eta, *strips = pl.pallas_call(
        functools.partial(join_kernel, chunk_rows),
        grid=(consts,),
        in_specs=[
            SMEM,
            fields(2, 0),
            fields(2, 2),
            fields(2, 4),
            plane,
            plane,
            half_re,
            half_im,
        ],
        out_specs=[fields(2, 0)] + strip_specs,
        out_shape=[jax.ShapeDtypeStruct((2,) + state.shape[1:], f32)] + strip_shapes,
        compiler_params=params(32),
        cost_estimate=cost(10**6, 6 * 10**6),
    )(omega, state, state, state, water_depth, ocean_mask, forcing, forcing)
    state, strips = sweep(eta, state, exchange(strips), forcing, True)
    state, _ = sweep(state, state, exchange(strips), forcing, False)
    return state.reshape(tide_state.shape)


def solution(mesh):
    placed = (
        P(None, "lat", "lon"),
        P(None, "lat", "lon"),
        P("lat", "lon"),
        P("lat", "lon"),
        P("lat", "lon"),
        P(None, ("lat", "lon")),
        P(("lat", "lon"), None),
        P(("lat", "lon")),
    )
    return jax.shard_map(
        local, mesh=mesh, in_specs=placed, out_specs=P(None, "lat", "lon"), check_vma=False
    )
```

```python
import functools

import jax
import jax.numpy as jnp
from jax import lax
from jax.experimental import pallas as pl
from jax.experimental.pallas import tpu as pltpu
from jax.sharding import PartitionSpec as P

OMEGAS = [1.405, 1.454, 1.379, 1.458, 0.729, 0.676, 0.725, 0.649]
RELAX = 0.8
LANES = 128
BLOCK = 256
SPAN = 2048
SUM_SPAN = 1024
CUT_BITS = 11
HEAD = 8
MIB = 1 << 20
NT = (((1,), (1,)), ((), ()))
NN = (((1,), (0,)), ((), ()))
VMEM = pl.BlockSpec(memory_space=pltpu.VMEM)
SMEM = pl.BlockSpec(memory_space=pltpu.SMEM)
ANY = pl.BlockSpec(memory_space=pl.ANY)


def iota(shape, dim):
    return lax.broadcasted_iota(jnp.int32, shape, dim)


def params(mib):
    return pltpu.CompilerParams(vmem_limit_bytes=mib * MIB)


def cost(flops, nbytes):
    return pl.CostEstimate(flops=flops, bytes_accessed=nbytes, transcendentals=0)


def rank_kernel(tiles, cuts, group, dest_ref, cell_ref, *outs):
    slot_ref, table_ref = outs
    blocks, block = dest_ref.shape[0] // 2, BLOCK

    def lines(ref):
        return jnp.concatenate(
            [ref[pl.ds(side, blocks, stride=2), :] for side in range(2)], axis=1
        )

    tile = lines(dest_ref) ^ lax.axis_index("lon")
    keys = tile * cuts + ((lines(cell_ref) >> CUT_BITS) & (cuts - 1))
    upper = (iota((block, block), 0) < iota((block, block), 1)).astype(jnp.bfloat16)
    lane = iota((blocks, LANES), 1)
    slot = jnp.zeros((blocks, block), jnp.float32)
    base = jnp.zeros((blocks, 1), jnp.float32)
    counts = jnp.zeros((blocks, LANES), jnp.float32)
    bases = jnp.zeros((blocks, LANES), jnp.float32)
    for key in range(tiles * cuts):
        mine = keys == key
        ones = jnp.where(mine, 1.0, 0.0)
        before = lax.dot_general(
            ones.astype(jnp.bfloat16), upper, NN, preferred_element_type=jnp.float32
        )
        slot = slot + jnp.where(mine, before + base, 0.0)
        count = jnp.sum(ones, axis=1, keepdims=True)
        counts = jnp.where(lane == key, count, counts)
        bases = jnp.where(lane == key, base, bases)
        base = base + count
    lower = (iota((blocks, blocks), 1) < iota((blocks, blocks), 0)).astype(jnp.bfloat16)
    places = lax.dot_general(
        lower, counts.astype(jnp.bfloat16), NN, preferred_element_type=jnp.float32
    )
    total = jnp.broadcast_to(jnp.sum(counts, axis=0, keepdims=True), (8, LANES))
    first = jnp.zeros((8, LANES), jnp.float32)
    for back in range(1, cuts):
        inside = (iota((8, LANES), 1) & (cuts - 1)) >= back
        first = first + jnp.where(inside, pltpu.roll(total, back, 1), 0.0)
    most = jnp.max(counts, axis=1, keepdims=True)
    slot_ref[...] = slot.astype(jnp.int32)
    table_ref[:blocks, :] = jnp.where(lane == LANES - 1, most, counts).astype(jnp.int32)
    table_ref[blocks : 2 * blocks, :] = bases.astype(jnp.int32)
    table_ref[2 * blocks : 3 * blocks, :] = (places + first[0:1]).astype(jnp.int32)
    line, column = iota((8, LANES), 0), iota((8, LANES), 1)
    for part in range(blocks // group):
        largest = jnp.max(most[part * group : (part + 1) * group, :], axis=0, keepdims=True)
        total = jnp.where((line == 1) & (column == part), largest, total)
    table_ref[3 * blocks :, :] = total.astype(jnp.int32)


def bucket_kernel(tiles, cuts, capacity, width, group, table_ref, *refs):
    slot_ref, cell_ref, rows_any = refs[:3]
    outs = refs[3 : 3 + tiles]
    staged, held, turned, rows_ref, read_sem, write_sem = refs[3 + tiles :]
    keys = tiles * cuts
    blocks = slot_ref.shape[0]
    windows = capacity // LANES
    room = capacity + BLOCK
    chunk = 32
    inside = iota((chunk, LANES), 0)
    row_of = iota((BLOCK, BLOCK), 0)
    third = iota((16, BLOCK), 0)
    pad = jnp.zeros((LANES - 2 * width - 16, BLOCK), jnp.bfloat16)

    def permute(at, first):
        block = first + at
        slot = slot_ref[pl.ds(block, 1), :]
        cell = jnp.concatenate(
            [cell_ref[pl.ds(2 * block + side, 1), :] for side in range(2)], axis=1
        )
        rows = rows_ref[:, pl.ds(pl.multiple_of(block * BLOCK, BLOCK), BLOCK)]
        high = rows.astype(jnp.bfloat16)
        low = (rows - high.astype(jnp.float32)).astype(jnp.bfloat16)
        cells = jnp.where(
            third == 0, cell >> 7, jnp.where(third == 1, cell & 127, 0)
        ).astype(jnp.float32)
        payload = jnp.concatenate([high, low, cells.astype(jnp.bfloat16), pad], axis=0)
        onehot = jnp.where(row_of == slot, 1.0, 0.0).astype(jnp.bfloat16)
        staged[pl.ds(pl.multiple_of(at * BLOCK, BLOCK), BLOCK), :] = lax.dot_general(
            onehot, payload, NT, preferred_element_type=jnp.float32
        )
        return first

    def move(at, block, key, part):
        count = table_ref[block, key]
        source = at * BLOCK + table_ref[blocks + block, key] + part * chunk
        place = (key // cuts) * room + table_ref[2 * blocks + block, key] + part * chunk
        pltpu.store(
            held.at[pl.ds(place, chunk), :],
            staged[pl.ds(source, chunk), :],
            mask=inside < count - part * chunk,
        )

    def spread(at, first):
        for key in range(keys):
            move(at, first + at, key, 0)
        return first

    def spread_rest(at, first):
        block = first + at

        @pl.when(table_ref[block, LANES - 1] > chunk)
        def _more():
            for key in range(keys):

                def step(part, carry, key=key):
                    move(at, block, key, part)
                    return carry

                lax.fori_loop(1, pl.cdiv(table_ref[block, key], chunk), step, 0)

        return first

    span = group * BLOCK
    reads = [
        pltpu.make_async_copy(
            rows_any.at[:, part * span : (part + 1) * span],
            rows_ref.at[:, part * span : (part + 1) * span],
            read_sem.at[part],
        )
        for part in range(blocks // group)
    ]
    for read in reads:
        read.start()
    for part in range(blocks // group):
        reads[part].wait()
        lax.fori_loop(0, group, permute, part * group, unroll=16)
        lax.fori_loop(0, group, spread, part * group, unroll=4)

        @pl.when(table_ref[3 * blocks + 1, part] > chunk)
        def _long(part=part):
            lax.fori_loop(0, group, spread_rest, part * group)

    row, lane = iota((32, LANES), 0), iota((32, LANES), 1)
    joined = jnp.where((row < width) & ((lane == row) | (lane == row + width)), 1.0, 0.0)
    joined = joined + jnp.where((row == width) & (lane == 2 * width), 128.0, 0.0)
    joined = joined + jnp.where((row == width) & (lane == 2 * width + 1), 1.0, 0.0)
    joined = joined.astype(jnp.bfloat16)
    lanes = iota((1, BLOCK), 1)
    writes = []
    for tile in range(tiles):
        out = turned.at[tile]
        sizes = [table_ref[3 * blocks, tile * cuts + cut] for cut in range(cuts)]
        count = functools.reduce(lambda a, b: a + b, sizes)

        def turn(part, carry, tile=tile, count=count, out=out):
            for piece in range(SPAN // BLOCK):
                first = part * SPAN + piece * BLOCK
                block = held[pl.ds(pl.multiple_of(tile * room + first, 8), BLOCK), :]
                both = lax.dot_general(
                    joined, block.astype(jnp.bfloat16), NT, preferred_element_type=jnp.float32
                )
                cells = jnp.where(lanes + first < count, both[width : width + 1], -1.0)
                for side in range(BLOCK // LANES):
                    at = part * (SPAN // LANES) + piece * (BLOCK // LANES) + side
                    cut = slice(side * LANES, (side + 1) * LANES)
                    out[pl.ds(pl.multiple_of(at * width, width), width), :] = both[:width, cut]
                    out[pl.ds(windows * width + at, 1), :] = cells[:, cut]
            return carry

        lax.fori_loop(0, pl.cdiv(count, SPAN), turn, 0)
        line = iota((HEAD, LANES), 0)
        head = jnp.zeros((HEAD, LANES), jnp.int32)
        for cut in range(cuts):
            head = jnp.where(line == cut, sizes[cut], head)
        out[windows * (width + 1) :, :] = head.astype(jnp.float32)
        writes.append(pltpu.make_async_copy(out, outs[tile], write_sem.at[tile]))
        writes[-1].start()
    for write in writes:
        write.wait()


def sum_kernel(width, windows, amount, cuts, fresh, *refs):
    buckets = refs[:amount]
    out = refs[-1]
    half, wide = out.shape[1:]
    high_of = half // cuts
    chunk = SUM_SPAN
    if fresh:
        out[...] = jnp.zeros_like(out)
    else:
        out[...] = refs[amount][...]
    row_of = iota((high_of, chunk), 0)
    col_of = iota((wide, chunk), 0)
    lanes = iota((1, LANES), 1)
    for bucket in buckets:
        top = windows * (width + 1)
        sizes = [
            jnp.max(bucket[top + cut : top + cut + 1, :]).astype(jnp.int32) for cut in range(cuts)
        ]
        total = functools.reduce(lambda a, b: a + b, sizes)
        start = jnp.int32(0)
        for cut in range(cuts):
            first = start // LANES
            start = start + sizes[cut]

            def step(part, carry, bucket=bucket, cut=cut, first=first):
                vals, cells = [], []
                for side in range(chunk // LANES):
                    at = first + part * (chunk // LANES) + side
                    read = jnp.minimum(at, windows - 1)
                    vals.append(bucket[pl.ds(pl.multiple_of(read * width, width), width), :])
                    cell = bucket[pl.ds(windows * width + read, 1), :]
                    cells.append(jnp.where(at * LANES + lanes < total, cell, -1.0))
                rows = jnp.concatenate(vals, axis=1)
                cell = jnp.concatenate(cells, axis=1).astype(jnp.int32)
                grid_row = cell >> 7
                low_row = jnp.where(cell < 0, -1, (grid_row & (half - 1)) - cut * high_of)
                column = (cell & 127) + jnp.where(grid_row >= half, LANES, 0)
                high = rows.astype(jnp.bfloat16)
                low = (rows - high.astype(jnp.float32)).astype(jnp.bfloat16)
                mine = row_of == low_row
                onehot = jnp.where(col_of == column, 1.0, 0.0).astype(jnp.bfloat16)
                left = []
                for channel in range(width):
                    one = slice(channel, channel + 1)
                    left.append(
                        jnp.concatenate(
                            [
                                jnp.where(mine, high[one].astype(jnp.float32), 0.0),
                                jnp.where(mine, low[one].astype(jnp.float32), 0.0),
                            ],
                            axis=1,
                        ).astype(jnp.bfloat16)
                    )
                product = lax.dot_general(
                    jnp.concatenate(left, axis=0),
                    jnp.concatenate([onehot, onehot], axis=1),
                    NT,
                    preferred_element_type=jnp.float32,
                )
                part_of = slice(cut * high_of, (cut + 1) * high_of)
                out[:, part_of, :] += product.reshape(width, high_of, wide)
                return carry

            lax.fori_loop(0, pl.cdiv(start - first * LANES, chunk), step, 0)


def put_edges(strips, k, rows, r0, last_row, fields):
    north, south, west, east = strips
    eta_re, eta_im, east_re, east_im, north_re, north_im = fields
    lane = iota((rows, LANES), 1)
    part = pl.ds(r0, rows)
    for group, field in enumerate((eta_re, eta_im, east_re, east_im)):
        at = group * 8 + k
        west[part, :] = jnp.where(lane == at, pltpu.roll(field, at, 1), west[part, :])
        east[part, :] = jnp.where(lane == at, pltpu.roll(field, at + 1, 1), east[part, :])
    for group, field in enumerate((eta_re, eta_im, north_re, north_im)):
        at = group * 8 + k
        if r0 == 0:
            north[pl.ds(at, 1), :] = field[0:1]
        if r0 + rows == last_row:
            south[pl.ds(at, 1), :] = field[rows - 1 : rows]


def edges_kernel(per, rows, state_ref, depth_ref, *strips):
    for kk in range(per):
        edges_at(pl.program_id(0) * per + kk, kk, rows, state_ref, depth_ref, *strips)


def edges_at(k, kk, rows, state_ref, depth_ref, *strips):
    height = depth_ref.shape[0]
    for r0 in range(0, height, rows):
        part = slice(r0, r0 + rows)
        depth = depth_ref[part, :]
        fields = [state_ref[g, kk, part, :] for g in range(6)]
        fields = fields[:2] + [depth * field for field in fields[2:]]
        put_edges(strips, k, rows, r0, height, fields)


def force(force_ref, channel, r0, rows, half):
    side = r0 // half
    at = r0 % half
    return force_ref[channel, at : at + rows, side * LANES : (side + 1) * LANES]


def join_kernel(per, rows, omega_ref, eta_ref, east_ref, north_ref, depth_ref, ocean_ref, re_ref, im_ref, out_ref, *strips):
    for kk in range(per):
        join_at(pl.program_id(0) * per + kk, kk, rows, omega_ref, eta_ref, east_ref, north_ref, depth_ref, ocean_ref, re_ref, im_ref, out_ref, *strips)


def join_at(k, kk, rows, omega_ref, eta_ref, east_ref, north_ref, depth_ref, ocean_ref, re_ref, im_ref, out_ref, *strips):
    omega = omega_ref[k]
    weight = RELAX / (1.0 + omega * omega)
    height = depth_ref.shape[0]
    for r0 in range(0, height, rows):
        part = slice(r0, r0 + rows)
        depth = depth_ref[part, :]
        ocean = ocean_ref[part, :].astype(jnp.float32) * weight
        f_re = force(re_ref, kk, r0, rows, height // 2)
        f_im = force(im_ref, kk, r0, rows, height // 2)
        eta_re = eta_ref[0, kk, part, :] + ocean * (f_re + f_im * omega)
        eta_im = eta_ref[1, kk, part, :] + ocean * (f_im - f_re * omega)
        out_ref[0, kk, part, :] = eta_re
        out_ref[1, kk, part, :] = eta_im
        fields = [eta_re, eta_im] + [
            depth * ref[g, kk, part, :] for ref in (east_ref, north_ref) for g in range(2)
        ]
        put_edges(strips, k, rows, r0, height, fields)


def sweep_kernel(per, rows, forced, edges, *refs):
    for kk in range(per):
        sweep_at(pl.program_id(0) * per + kk, kk, rows, forced, edges, *refs)


def sweep_at(k, kk, rows, forced, edges, *refs):
    refs = list(refs)
    omega_ref, eta_ref, vel_e_ref, vel_n_ref, pot_ref = refs[:5]
    depth_ref, drag_ref, ocean_ref, turn_ref = refs[5:9]
    north_in, south_in, west_in, east_in = refs[9:13]
    refs = refs[13:]
    if forced:
        re_ref, im_ref = refs[:2]
        refs = refs[2:]
    out_ref = refs[0]
    strips = refs[1:]
    omega = omega_ref[k]
    inv_eta = 1.0 / (1.0 + omega * omega)
    height = depth_ref.shape[0]
    lane = iota((rows, LANES), 1)
    row = iota((rows, LANES), 0)

    def dlon(q, group, r0):
        at = group * 8 + k
        part = slice(r0, r0 + rows)
        left = pltpu.roll(q, 1, 1)
        right = pltpu.roll(q, LANES - 1, 1)
        w = pltpu.roll(west_in[part, :], (LANES - at) % LANES, 1)
        e = pltpu.roll(east_in[part, :], LANES - 1 - at, 1)
        return (jnp.where(lane == LANES - 1, e, right) - jnp.where(lane == 0, w, left)) * 0.5

    def shifted(q, first, last, group, r0):
        at = group * 8 + k
        above = first if r0 > 0 else north_in[pl.ds(at, 1), :]
        below = last if r0 + rows < height else south_in[pl.ds(at, 1), :]
        up = jnp.where(row == 0, above, pltpu.roll(q, 1, 0))
        down = jnp.where(row == rows - 1, below, pltpu.roll(q, rows - 1, 0))
        return (down - up) * 0.5

    for r0 in range(0, height, rows):
        part = slice(r0, r0 + rows)
        before = slice(max(r0 - 1, 0), max(r0 - 1, 0) + 1)
        after = slice(min(r0 + rows, height - 1), min(r0 + rows, height - 1) + 1)
        depth = depth_ref[part, :]
        diag = 1.0 + drag_ref[part, :]
        ocean = ocean_ref[part, :].astype(jnp.float32)
        turn = turn_ref[part, :]
        inv = 1.0 / (diag * diag + omega * omega)
        eta = [eta_ref[g, kk, part, :] for g in range(2)]
        east = [vel_e_ref[g, kk, part, :] for g in range(2)]
        north = [vel_n_ref[g, kk, part, :] for g in range(2)]
        pot = [pot_ref[g, kk, part, :] for g in range(6)]
        flux = []
        grad_lat = []
        for g in range(2):
            hn = depth * north[g]
            hn_first = depth_ref[before, :] * vel_n_ref[g, kk, before, :]
            hn_last = depth_ref[after, :] * vel_n_ref[g, kk, after, :]
            flux.append(
                dlon(depth * east[g], 2 + g, r0) + shifted(hn, hn_first, hn_last, 2 + g, r0)
            )
            grad_lat.append(
                shifted(eta[g], eta_ref[g, kk, before, :], eta_ref[g, kk, after, :], g, r0)
            )
        grad_lon = [dlon(eta[g], g, r0) for g in range(2)]
        res_re = pot[0] - (eta[0] - omega * eta[1] + flux[0])
        res_im = pot[1] - (eta[1] + omega * eta[0] + flux[1])
        if forced:
            res_re = res_re + force(re_ref, kk, r0, rows, height // 2)
            res_im = res_im + force(im_ref, kk, r0, rows, height // 2)
        weight = ocean * RELAX
        new = [
            ocean * eta[0] + weight * ((res_re + res_im * omega) * inv_eta),
            ocean * eta[1] + weight * ((res_im - res_re * omega) * inv_eta),
        ]
        scaled = weight * inv
        for own, other, grad, at, sign in (
            (east, north, grad_lon, 2, -1.0),
            (north, east, grad_lat, 4, 1.0),
        ):
            spun = [sign * (turn * other[g]) for g in range(2)]
            res_re = pot[at] - (diag * own[0] - omega * own[1] + spun[0] + grad[0])
            res_im = pot[at + 1] - (diag * own[1] + omega * own[0] + spun[1] + grad[1])
            new.append(ocean * own[0] + scaled * (res_re * diag + res_im * omega))
            new.append(ocean * own[1] + scaled * (res_im * diag - res_re * omega))
        for g in range(6):
            out_ref[g, kk, part, :] = new[g]
        if edges:
            put_edges(strips, k, rows, r0, height, new[:2] + [depth * q for q in new[2:]])


def local(
    tide_state, potential, water_depth, drag_coeff, ocean_mask, residual_rows, dest_tile, dest_cell
):
    f32 = jnp.float32
    tiles = lax.axis_size("lon")
    lats = lax.axis_size("lat")
    width, row_count = residual_rows.shape
    capacity = 2 * row_count // tiles
    height, across = water_depth.shape
    consts = tide_state.shape[0] // 6
    blocks = row_count // BLOCK
    windows = capacity // LANES
    cuts = max(1, min(4, 32 // tiles))
    cells = dest_cell.reshape(2 * blocks, LANES)
    bucket_rows = windows * (width + 1) + HEAD

    group = min(32, blocks)
    omega = jnp.asarray(OMEGAS, f32)
    row_ids = lax.axis_index("lat") * height + jnp.arange(height, dtype=jnp.int32)
    lat_pos = (row_ids.astype(f32) + 0.5) / (height * lats) - 0.5
    turn = jnp.broadcast_to((0.5 * jnp.sin(jnp.pi * lat_pos))[:, None], (height, across))

    state = tide_state.reshape(6, consts, height, across)
    pot = potential.reshape(6, consts, height, across)
    chunk_rows, per = 64, 4

    def fields(count, first):
        return pl.BlockSpec((count, per, height, across), lambda k: (first // count, k, 0, 0))

    plane = pl.BlockSpec((height, across), lambda k: (0, 0))
    flat = pl.BlockSpec((4 * consts, across), lambda k: (0, 0))
    half_re = pl.BlockSpec((per, height // 2, 2 * across), lambda k: (k, 0, 0))
    half_im = pl.BlockSpec((per, height // 2, 2 * across), lambda k: (consts // per + k, 0, 0))
    strip_specs = [flat, flat, plane, plane]
    strip_shapes = [jax.ShapeDtypeStruct((4 * consts, across), f32)] * 2 + [
        jax.ShapeDtypeStruct((height, across), f32)
    ] * 2
    state_shape = jax.ShapeDtypeStruct(state.shape, f32)

    def exchange(strips):
        north, south, west, east = strips
        return (
            lax.ppermute(south, "lat", [(i, i + 1) for i in range(lats - 1)]),
            lax.ppermute(north, "lat", [(i + 1, i) for i in range(lats - 1)]),
            lax.ppermute(east, "lon", [(i, (i + 1) % tiles) for i in range(tiles)]),
            lax.ppermute(west, "lon", [((i + 1) % tiles, i) for i in range(tiles)]),
        )

    def sweep(eta, vel, strips, forcing, edges):
        forced = forcing is not None
        out = pl.pallas_call(
            functools.partial(sweep_kernel, per, chunk_rows, forced, edges),
            grid=(consts // per,),
            in_specs=[SMEM, fields(2, 0), fields(2, 2), fields(2, 4), fields(6, 0)]
            + [plane] * 4
            + strip_specs
            + ([half_re, half_im] if forced else []),
            out_specs=[fields(6, 0)] + (strip_specs if edges else []),
            out_shape=[state_shape] + (strip_shapes if edges else []),
            compiler_params=params(32),
            cost_estimate=cost(16 * 10**6, 9 * 10**6),
        )(
            omega, eta, vel, vel, pot, water_depth, drag_coeff, ocean_mask, turn, *strips,
            *((forcing, forcing) if forced else ()),
        )
        return out[0], out[1:]

    slot, table = pl.pallas_call(
        functools.partial(rank_kernel, tiles, cuts, group),
        in_specs=[VMEM, VMEM],
        out_specs=[VMEM] * 2,
        out_shape=[
            jax.ShapeDtypeStruct((blocks, BLOCK), jnp.int32),
            jax.ShapeDtypeStruct((3 * blocks + 8, LANES), jnp.int32),
        ],
        compiler_params=params(32),
    )(dest_tile.reshape(2 * blocks, LANES), cells)

    strips = pl.pallas_call(
        functools.partial(edges_kernel, per, chunk_rows),
        grid=(consts // per,),
        in_specs=[fields(6, 0), plane],
        out_specs=strip_specs,
        out_shape=strip_shapes,
        compiler_params=params(32),
        cost_estimate=cost(10**6, 3 * 10**6),
    )(state, water_depth)
    strips = exchange(strips)


    buckets = pl.pallas_call(
        functools.partial(bucket_kernel, tiles, cuts, capacity, width, group),
        in_specs=[SMEM, VMEM, VMEM, ANY],
        out_specs=[ANY] * tiles,
        out_shape=[jax.ShapeDtypeStruct((bucket_rows, LANES), f32)] * tiles,
        scratch_shapes=[
            pltpu.VMEM(((group + 1) * BLOCK, LANES), f32),
            pltpu.VMEM((tiles * (capacity + BLOCK), LANES), f32),
            pltpu.VMEM((tiles, bucket_rows, LANES), f32),
            pltpu.VMEM((width, row_count), f32),
            pltpu.SemaphoreType.DMA((blocks // group,)),
            pltpu.SemaphoreType.DMA((tiles,)),
        ],
        compiler_params=params(60),
        cost_estimate=cost(10**10, 7 * 10**6),
    )(table, slot, cells, residual_rows)

    grid_shape = jax.ShapeDtypeStruct((width, height // 2, 2 * across), f32)

    def add(parts, total):
        return pl.pallas_call(
            functools.partial(sum_kernel, width, windows, len(parts), cuts, total is None),
            in_specs=[VMEM] * (len(parts) + (total is not None)),
            out_specs=VMEM,
            out_shape=grid_shape,
            compiler_params=params(40),
            cost_estimate=cost(10**10, 3 * 10**6),
        )(*parts, *(() if total is None else (total,)))

    half = tiles // 2
    order = [half] + list(range(1, half)) + list(range(half + 1, tiles))
    arrived = [
        lax.ppermute(buckets[s], "lon", [(i, i ^ s) for i in range(tiles)]) for s in order
    ]
    state, _ = sweep(state, state, strips, None, False)
    forcing = add([buckets[0]], None)
    each = tiles // 8
    for first in range(0, len(arrived), each):
        forcing = add(arrived[first : first + each], forcing)

    eta, *strips = pl.pallas_call(
        functools.partial(join_kernel, per, chunk_rows),
        grid=(consts // per,),
        in_specs=[
            SMEM,
            fields(2, 0),
            fields(2, 2),
            fields(2, 4),
            plane,
            plane,
            half_re,
            half_im,
        ],
        out_specs=[fields(2, 0)] + strip_specs,
        out_shape=[jax.ShapeDtypeStruct((2,) + state.shape[1:], f32)] + strip_shapes,
        compiler_params=params(32),
        cost_estimate=cost(10**6, 6 * 10**6),
    )(omega, state, state, state, water_depth, ocean_mask, forcing, forcing)
    state, strips = sweep(eta, state, exchange(strips), forcing, True)
    state, _ = sweep(state, state, exchange(strips), forcing, False)
    return state.reshape(tide_state.shape)


def solution(mesh):
    placed = (
        P(None, "lat", "lon"),
        P(None, "lat", "lon"),
        P("lat", "lon"),
        P("lat", "lon"),
        P("lat", "lon"),
        P(None, ("lat", "lon")),
        P(("lat", "lon"), None),
        P(("lat", "lon")),
    )
    return jax.shard_map(
        local, mesh=mesh, in_specs=placed, out_specs=P(None, "lat", "lon"), check_vma=False
    )
```

```python
import functools

import jax
import jax.numpy as jnp
from jax import lax
from jax.experimental import pallas as pl
from jax.experimental.pallas import tpu as pltpu
from jax.sharding import PartitionSpec as P

OMEGAS = [1.405, 1.454, 1.379, 1.458, 0.729, 0.676, 0.725, 0.649]
RELAX = 0.8
LANES = 128
BLOCK = 256
SPAN = 2048
SUM_SPAN = 1024
CUT_BITS = 11
HEAD = 8
MIB = 1 << 20
NT = (((1,), (1,)), ((), ()))
NN = (((1,), (0,)), ((), ()))
VMEM = pl.BlockSpec(memory_space=pltpu.VMEM)
SMEM = pl.BlockSpec(memory_space=pltpu.SMEM)
ANY = pl.BlockSpec(memory_space=pl.ANY)


def iota(shape, dim):
    return lax.broadcasted_iota(jnp.int32, shape, dim)


def params(mib):
    return pltpu.CompilerParams(vmem_limit_bytes=mib * MIB)


def cost(flops, nbytes):
    return pl.CostEstimate(flops=flops, bytes_accessed=nbytes, transcendentals=0)


def rank(tiles, cuts, group, dest_ref, cell_ref, slot_ref, table_ref):
    blocks, block = dest_ref.shape[0] // 2, BLOCK

    def lines(ref):
        return jnp.concatenate(
            [ref[pl.ds(side, blocks, stride=2), :] for side in range(2)], axis=1
        )

    tile = lines(dest_ref) ^ lax.axis_index("lon")
    keys = tile * cuts + ((lines(cell_ref) >> CUT_BITS) & (cuts - 1))
    upper = (iota((block, block), 0) < iota((block, block), 1)).astype(jnp.bfloat16)
    lane = iota((blocks, LANES), 1)
    slot = jnp.zeros((blocks, block), jnp.float32)
    base = jnp.zeros((blocks, 1), jnp.float32)
    counts = jnp.zeros((blocks, LANES), jnp.float32)
    bases = jnp.zeros((blocks, LANES), jnp.float32)
    for key in range(tiles * cuts):
        mine = keys == key
        ones = jnp.where(mine, 1.0, 0.0)
        before = lax.dot_general(
            ones.astype(jnp.bfloat16), upper, NN, preferred_element_type=jnp.float32
        )
        slot = slot + jnp.where(mine, before + base, 0.0)
        count = jnp.sum(ones, axis=1, keepdims=True)
        counts = jnp.where(lane == key, count, counts)
        bases = jnp.where(lane == key, base, bases)
        base = base + count
    lower = (iota((blocks, blocks), 1) < iota((blocks, blocks), 0)).astype(jnp.bfloat16)
    places = lax.dot_general(
        lower, counts.astype(jnp.bfloat16), NN, preferred_element_type=jnp.float32
    )
    total = jnp.broadcast_to(jnp.sum(counts, axis=0, keepdims=True), (8, LANES))
    first = jnp.zeros((8, LANES), jnp.float32)
    for back in range(1, cuts):
        inside = (iota((8, LANES), 1) & (cuts - 1)) >= back
        first = first + jnp.where(inside, pltpu.roll(total, back, 1), 0.0)
    most = jnp.max(counts, axis=1, keepdims=True)
    slot_ref[...] = slot.astype(jnp.int32)
    table_ref[:blocks, :] = jnp.where(lane == LANES - 1, most, counts).astype(jnp.int32)
    table_ref[blocks : 2 * blocks, :] = bases.astype(jnp.int32)
    table_ref[2 * blocks : 3 * blocks, :] = (places + first[0:1]).astype(jnp.int32)
    line, column = iota((8, LANES), 0), iota((8, LANES), 1)
    for part in range(blocks // group):
        largest = jnp.max(most[part * group : (part + 1) * group, :], axis=0, keepdims=True)
        total = jnp.where((line == 1) & (column == part), largest, total)
    table_ref[3 * blocks :, :] = total.astype(jnp.int32)


def bucket_kernel(tiles, cuts, capacity, width, group, *refs):
    dest_ref, cell_ref, rows_any = refs[:3]
    outs = refs[3 : 3 + tiles]
    staged, held, turned, rows_ref, slot_ref, table_held, table_ref = refs[3 + tiles : 10 + tiles]
    read_sem, write_sem, table_sem = refs[10 + tiles :]
    keys = tiles * cuts
    blocks = slot_ref.shape[0]
    windows = capacity // LANES
    room = capacity + BLOCK
    chunk = 32
    inside = iota((chunk, LANES), 0)
    row_of = iota((BLOCK, BLOCK), 0)
    third = iota((16, BLOCK), 0)
    pad = jnp.zeros((LANES - 2 * width - 16, BLOCK), jnp.bfloat16)

    def permute(at, first):
        block = first + at
        slot = slot_ref[pl.ds(block, 1), :]
        cell = jnp.concatenate(
            [cell_ref[pl.ds(2 * block + side, 1), :] for side in range(2)], axis=1
        )
        rows = rows_ref[:, pl.ds(pl.multiple_of(block * BLOCK, BLOCK), BLOCK)]
        high = rows.astype(jnp.bfloat16)
        low = (rows - high.astype(jnp.float32)).astype(jnp.bfloat16)
        cells = jnp.where(
            third == 0, cell >> 7, jnp.where(third == 1, cell & 127, 0)
        ).astype(jnp.float32)
        payload = jnp.concatenate([high, low, cells.astype(jnp.bfloat16), pad], axis=0)
        onehot = jnp.where(row_of == slot, 1.0, 0.0).astype(jnp.bfloat16)
        staged[pl.ds(pl.multiple_of(at * BLOCK, BLOCK), BLOCK), :] = lax.dot_general(
            onehot, payload, NT, preferred_element_type=jnp.float32
        )
        return first

    def move(at, block, key, part):
        count = table_ref[block, key]
        source = at * BLOCK + table_ref[blocks + block, key] + part * chunk
        place = (key // cuts) * room + table_ref[2 * blocks + block, key] + part * chunk
        pltpu.store(
            held.at[pl.ds(place, chunk), :],
            staged[pl.ds(source, chunk), :],
            mask=inside < count - part * chunk,
        )

    def spread(at, first):
        for key in range(keys):
            move(at, first + at, key, 0)
        return first

    def spread_rest(at, first):
        block = first + at

        @pl.when(table_ref[block, LANES - 1] > chunk)
        def _more():
            for key in range(keys):

                def step(part, carry, key=key):
                    move(at, block, key, part)
                    return carry

                lax.fori_loop(1, pl.cdiv(table_ref[block, key], chunk), step, 0)

        return first

    span = group * BLOCK
    reads = [
        pltpu.make_async_copy(
            rows_any.at[:, part * span : (part + 1) * span],
            rows_ref.at[:, part * span : (part + 1) * span],
            read_sem.at[part],
        )
        for part in range(blocks // group)
    ]
    for read in reads:
        read.start()
    rank(tiles, cuts, group, dest_ref, cell_ref, slot_ref, table_held)
    tabled = pltpu.make_async_copy(table_held, table_ref, table_sem)
    tabled.start()
    tabled.wait()
    for part in range(blocks // group):
        reads[part].wait()
        lax.fori_loop(0, group, permute, part * group, unroll=32)
        lax.fori_loop(0, group, spread, part * group, unroll=4)

        @pl.when(table_ref[3 * blocks + 1, part] > chunk)
        def _long(part=part):
            lax.fori_loop(0, group, spread_rest, part * group)

    row, lane = iota((32, LANES), 0), iota((32, LANES), 1)
    joined = jnp.where((row < width) & ((lane == row) | (lane == row + width)), 1.0, 0.0)
    joined = joined + jnp.where((row == width) & (lane == 2 * width), 128.0, 0.0)
    joined = joined + jnp.where((row == width) & (lane == 2 * width + 1), 1.0, 0.0)
    joined = joined.astype(jnp.bfloat16)
    lanes = iota((1, BLOCK), 1)
    writes = []
    for tile in range(tiles):
        out = turned.at[tile]
        sizes = [table_ref[3 * blocks, tile * cuts + cut] for cut in range(cuts)]
        count = functools.reduce(lambda a, b: a + b, sizes)

        def turn(part, carry, tile=tile, count=count, out=out):
            for piece in range(SPAN // BLOCK):
                first = part * SPAN + piece * BLOCK
                block = held[pl.ds(pl.multiple_of(tile * room + first, 8), BLOCK), :]
                both = lax.dot_general(
                    joined, block.astype(jnp.bfloat16), NT, preferred_element_type=jnp.float32
                )
                cells = jnp.where(lanes + first < count, both[width : width + 1], -1.0)
                for side in range(BLOCK // LANES):
                    at = part * (SPAN // LANES) + piece * (BLOCK // LANES) + side
                    cut = slice(side * LANES, (side + 1) * LANES)
                    out[pl.ds(pl.multiple_of(at * width, width), width), :] = both[:width, cut]
                    out[pl.ds(windows * width + at, 1), :] = cells[:, cut]
            return carry

        lax.fori_loop(0, pl.cdiv(count, SPAN), turn, 0)
        line = iota((HEAD, LANES), 0)
        head = jnp.zeros((HEAD, LANES), jnp.int32)
        for cut in range(cuts):
            head = jnp.where(line == cut, sizes[cut], head)
        out[windows * (width + 1) :, :] = head.astype(jnp.float32)
        writes.append(pltpu.make_async_copy(out, outs[tile], write_sem.at[tile]))
        writes[-1].start()
    for write in writes:
        write.wait()


def sum_kernel(width, windows, amount, cuts, fresh, *refs):
    buckets = refs[:amount]
    out = refs[-1]
    half, wide = out.shape[1:]
    high_of = half // cuts
    chunk = SUM_SPAN
    if fresh:
        out[...] = jnp.zeros_like(out)
    else:
        out[...] = refs[amount][...]
    row_of = iota((high_of, chunk), 0)
    col_of = iota((wide, chunk), 0)
    lanes = iota((1, LANES), 1)
    for bucket in buckets:
        top = windows * (width + 1)
        sizes = [
            jnp.max(bucket[top + cut : top + cut + 1, :]).astype(jnp.int32) for cut in range(cuts)
        ]
        total = functools.reduce(lambda a, b: a + b, sizes)
        start = jnp.int32(0)
        for cut in range(cuts):
            first = start // LANES
            start = start + sizes[cut]

            def step(part, carry, bucket=bucket, cut=cut, first=first):
                vals, cells = [], []
                for side in range(chunk // LANES):
                    at = first + part * (chunk // LANES) + side
                    read = jnp.minimum(at, windows - 1)
                    vals.append(bucket[pl.ds(pl.multiple_of(read * width, width), width), :])
                    cell = bucket[pl.ds(windows * width + read, 1), :]
                    cells.append(jnp.where(at * LANES + lanes < total, cell, -1.0))
                rows = jnp.concatenate(vals, axis=1)
                cell = jnp.concatenate(cells, axis=1).astype(jnp.int32)
                grid_row = cell >> 7
                low_row = jnp.where(cell < 0, -1, (grid_row & (half - 1)) - cut * high_of)
                column = (cell & 127) + jnp.where(grid_row >= half, LANES, 0)
                high = rows.astype(jnp.bfloat16)
                low = (rows - high.astype(jnp.float32)).astype(jnp.bfloat16)
                mine = row_of == low_row
                onehot = jnp.where(col_of == column, 1.0, 0.0).astype(jnp.bfloat16)
                left = []
                for channel in range(width):
                    one = slice(channel, channel + 1)
                    left.append(
                        jnp.concatenate(
                            [
                                jnp.where(mine, high[one].astype(jnp.float32), 0.0),
                                jnp.where(mine, low[one].astype(jnp.float32), 0.0),
                            ],
                            axis=1,
                        ).astype(jnp.bfloat16)
                    )
                product = lax.dot_general(
                    jnp.concatenate(left, axis=0),
                    jnp.concatenate([onehot, onehot], axis=1),
                    NT,
                    preferred_element_type=jnp.float32,
                )
                part_of = slice(cut * high_of, (cut + 1) * high_of)
                out[:, part_of, :] += product.reshape(width, high_of, wide)
                return carry

            lax.fori_loop(0, pl.cdiv(start - first * LANES, chunk), step, 0)


def put_edges(strips, k, rows, r0, last_row, fields):
    north, south, west, east = strips
    eta_re, eta_im, east_re, east_im, north_re, north_im = fields
    lane = iota((rows, LANES), 1)
    part = pl.ds(r0, rows)
    for group, field in enumerate((eta_re, eta_im, east_re, east_im)):
        at = group * 8 + k
        west[part, :] = jnp.where(lane == at, pltpu.roll(field, at, 1), west[part, :])
        east[part, :] = jnp.where(lane == at, pltpu.roll(field, at + 1, 1), east[part, :])
    for group, field in enumerate((eta_re, eta_im, north_re, north_im)):
        at = group * 8 + k
        if r0 == 0:
            north[pl.ds(at, 1), :] = field[0:1]
        if r0 + rows == last_row:
            south[pl.ds(at, 1), :] = field[rows - 1 : rows]


def edges_kernel(per, rows, state_ref, depth_ref, *strips):
    for kk in range(per):
        edges_at(pl.program_id(0) * per + kk, kk, rows, state_ref, depth_ref, *strips)


def edges_at(k, kk, rows, state_ref, depth_ref, *strips):
    height = depth_ref.shape[0]
    for r0 in range(0, height, rows):
        part = slice(r0, r0 + rows)
        depth = depth_ref[part, :]
        fields = [state_ref[g, kk, part, :] for g in range(6)]
        fields = fields[:2] + [depth * field for field in fields[2:]]
        put_edges(strips, k, rows, r0, height, fields)


def force(force_ref, channel, r0, rows, half):
    side = r0 // half
    at = r0 % half
    return force_ref[channel, at : at + rows, side * LANES : (side + 1) * LANES]


def join_kernel(per, rows, omega_ref, eta_ref, east_ref, north_ref, depth_ref, ocean_ref, re_ref, im_ref, out_ref, *strips):
    for kk in range(per):
        join_at(pl.program_id(0) * per + kk, kk, rows, omega_ref, eta_ref, east_ref, north_ref, depth_ref, ocean_ref, re_ref, im_ref, out_ref, *strips)


def join_at(k, kk, rows, omega_ref, eta_ref, east_ref, north_ref, depth_ref, ocean_ref, re_ref, im_ref, out_ref, *strips):
    omega = omega_ref[k]
    weight = RELAX / (1.0 + omega * omega)
    height = depth_ref.shape[0]
    for r0 in range(0, height, rows):
        part = slice(r0, r0 + rows)
        depth = depth_ref[part, :]
        ocean = ocean_ref[part, :].astype(jnp.float32) * weight
        f_re = force(re_ref, kk, r0, rows, height // 2)
        f_im = force(im_ref, kk, r0, rows, height // 2)
        eta_re = eta_ref[0, kk, part, :] + ocean * (f_re + f_im * omega)
        eta_im = eta_ref[1, kk, part, :] + ocean * (f_im - f_re * omega)
        out_ref[0, kk, part, :] = eta_re
        out_ref[1, kk, part, :] = eta_im
        fields = [eta_re, eta_im] + [
            depth * ref[g, kk, part, :] for ref in (east_ref, north_ref) for g in range(2)
        ]
        put_edges(strips, k, rows, r0, height, fields)


def sweep_kernel(per, rows, forced, edges, *refs):
    for kk in range(per):
        sweep_at(pl.program_id(0) * per + kk, kk, rows, forced, edges, *refs)


def sweep_at(k, kk, rows, forced, edges, *refs):
    refs = list(refs)
    omega_ref, eta_ref, vel_e_ref, vel_n_ref, pot_ref = refs[:5]
    depth_ref, drag_ref, ocean_ref, turn_ref = refs[5:9]
    north_in, south_in, west_in, east_in = refs[9:13]
    refs = refs[13:]
    if forced:
        re_ref, im_ref = refs[:2]
        refs = refs[2:]
    out_ref = refs[0]
    strips = refs[1:]
    omega = omega_ref[k]
    inv_eta = 1.0 / (1.0 + omega * omega)
    height = depth_ref.shape[0]
    lane = iota((rows, LANES), 1)
    row = iota((rows, LANES), 0)

    def dlon(q, group, r0):
        at = group * 8 + k
        part = slice(r0, r0 + rows)
        left = pltpu.roll(q, 1, 1)
        right = pltpu.roll(q, LANES - 1, 1)
        w = pltpu.roll(west_in[part, :], (LANES - at) % LANES, 1)
        e = pltpu.roll(east_in[part, :], LANES - 1 - at, 1)
        return (jnp.where(lane == LANES - 1, e, right) - jnp.where(lane == 0, w, left)) * 0.5

    def shifted(q, first, last, group, r0):
        at = group * 8 + k
        above = first if r0 > 0 else north_in[pl.ds(at, 1), :]
        below = last if r0 + rows < height else south_in[pl.ds(at, 1), :]
        up = jnp.where(row == 0, above, pltpu.roll(q, 1, 0))
        down = jnp.where(row == rows - 1, below, pltpu.roll(q, rows - 1, 0))
        return (down - up) * 0.5

    for r0 in range(0, height, rows):
        part = slice(r0, r0 + rows)
        before = slice(max(r0 - 1, 0), max(r0 - 1, 0) + 1)
        after = slice(min(r0 + rows, height - 1), min(r0 + rows, height - 1) + 1)
        depth = depth_ref[part, :]
        diag = 1.0 + drag_ref[part, :]
        ocean = ocean_ref[part, :].astype(jnp.float32)
        turn = turn_ref[part, :]
        inv = 1.0 / (diag * diag + omega * omega)
        eta = [eta_ref[g, kk, part, :] for g in range(2)]
        east = [vel_e_ref[g, kk, part, :] for g in range(2)]
        north = [vel_n_ref[g, kk, part, :] for g in range(2)]
        pot = [pot_ref[g, kk, part, :] for g in range(6)]
        flux = []
        grad_lat = []
        for g in range(2):
            hn = depth * north[g]
            hn_first = depth_ref[before, :] * vel_n_ref[g, kk, before, :]
            hn_last = depth_ref[after, :] * vel_n_ref[g, kk, after, :]
            flux.append(
                dlon(depth * east[g], 2 + g, r0) + shifted(hn, hn_first, hn_last, 2 + g, r0)
            )
            grad_lat.append(
                shifted(eta[g], eta_ref[g, kk, before, :], eta_ref[g, kk, after, :], g, r0)
            )
        grad_lon = [dlon(eta[g], g, r0) for g in range(2)]
        res_re = pot[0] - (eta[0] - omega * eta[1] + flux[0])
        res_im = pot[1] - (eta[1] + omega * eta[0] + flux[1])
        if forced:
            res_re = res_re + force(re_ref, kk, r0, rows, height // 2)
            res_im = res_im + force(im_ref, kk, r0, rows, height // 2)
        weight = ocean * RELAX
        new = [
            ocean * eta[0] + weight * ((res_re + res_im * omega) * inv_eta),
            ocean * eta[1] + weight * ((res_im - res_re * omega) * inv_eta),
        ]
        scaled = weight * inv
        for own, other, grad, at, sign in (
            (east, north, grad_lon, 2, -1.0),
            (north, east, grad_lat, 4, 1.0),
        ):
            spun = [sign * (turn * other[g]) for g in range(2)]
            res_re = pot[at] - (diag * own[0] - omega * own[1] + spun[0] + grad[0])
            res_im = pot[at + 1] - (diag * own[1] + omega * own[0] + spun[1] + grad[1])
            new.append(ocean * own[0] + scaled * (res_re * diag + res_im * omega))
            new.append(ocean * own[1] + scaled * (res_im * diag - res_re * omega))
        for g in range(6):
            out_ref[g, kk, part, :] = new[g]
        if edges:
            put_edges(strips, k, rows, r0, height, new[:2] + [depth * q for q in new[2:]])


def local(
    tide_state, potential, water_depth, drag_coeff, ocean_mask, residual_rows, dest_tile, dest_cell
):
    f32 = jnp.float32
    tiles = lax.axis_size("lon")
    lats = lax.axis_size("lat")
    width, row_count = residual_rows.shape
    capacity = 2 * row_count // tiles
    height, across = water_depth.shape
    consts = tide_state.shape[0] // 6
    blocks = row_count // BLOCK
    windows = capacity // LANES
    cuts = max(1, min(4, 32 // tiles))
    cells = dest_cell.reshape(2 * blocks, LANES)
    bucket_rows = windows * (width + 1) + HEAD

    group = min(32, blocks)
    omega = jnp.asarray(OMEGAS, f32)
    row_ids = lax.axis_index("lat") * height + jnp.arange(height, dtype=jnp.int32)
    lat_pos = (row_ids.astype(f32) + 0.5) / (height * lats) - 0.5
    turn = jnp.broadcast_to((0.5 * jnp.sin(jnp.pi * lat_pos))[:, None], (height, across))

    state = tide_state.reshape(6, consts, height, across)
    pot = potential.reshape(6, consts, height, across)
    chunk_rows, per = 64, 4

    def fields(count, first):
        return pl.BlockSpec((count, per, height, across), lambda k: (first // count, k, 0, 0))

    plane = pl.BlockSpec((height, across), lambda k: (0, 0))
    flat = pl.BlockSpec((4 * consts, across), lambda k: (0, 0))
    half_re = pl.BlockSpec((per, height // 2, 2 * across), lambda k: (k, 0, 0))
    half_im = pl.BlockSpec((per, height // 2, 2 * across), lambda k: (consts // per + k, 0, 0))
    strip_specs = [flat, flat, plane, plane]
    strip_shapes = [jax.ShapeDtypeStruct((4 * consts, across), f32)] * 2 + [
        jax.ShapeDtypeStruct((height, across), f32)
    ] * 2
    state_shape = jax.ShapeDtypeStruct(state.shape, f32)

    def exchange(strips):
        north, south, west, east = strips
        return (
            lax.ppermute(south, "lat", [(i, i + 1) for i in range(lats - 1)]),
            lax.ppermute(north, "lat", [(i + 1, i) for i in range(lats - 1)]),
            lax.ppermute(east, "lon", [(i, (i + 1) % tiles) for i in range(tiles)]),
            lax.ppermute(west, "lon", [((i + 1) % tiles, i) for i in range(tiles)]),
        )

    def sweep(eta, vel, strips, forcing, edges):
        forced = forcing is not None
        out = pl.pallas_call(
            functools.partial(sweep_kernel, per, chunk_rows, forced, edges),
            grid=(consts // per,),
            in_specs=[SMEM, fields(2, 0), fields(2, 2), fields(2, 4), fields(6, 0)]
            + [plane] * 4
            + strip_specs
            + ([half_re, half_im] if forced else []),
            out_specs=[fields(6, 0)] + (strip_specs if edges else []),
            out_shape=[state_shape] + (strip_shapes if edges else []),
            compiler_params=params(32),
            cost_estimate=cost(16 * 10**6, 9 * 10**6),
        )(
            omega, eta, vel, vel, pot, water_depth, drag_coeff, ocean_mask, turn, *strips,
            *((forcing, forcing) if forced else ()),
        )
        return out[0], out[1:]

    strips = pl.pallas_call(
        functools.partial(edges_kernel, per, chunk_rows),
        grid=(consts // per,),
        in_specs=[fields(6, 0), plane],
        out_specs=strip_specs,
        out_shape=strip_shapes,
        compiler_params=params(32),
        cost_estimate=cost(10**6, 3 * 10**6),
    )(state, water_depth)
    strips = exchange(strips)


    buckets = pl.pallas_call(
        functools.partial(bucket_kernel, tiles, cuts, capacity, width, group),
        in_specs=[VMEM, VMEM, ANY],
        out_specs=[ANY] * tiles,
        out_shape=[jax.ShapeDtypeStruct((bucket_rows, LANES), f32)] * tiles,
        scratch_shapes=[
            pltpu.VMEM(((group + 1) * BLOCK, LANES), f32),
            pltpu.VMEM((tiles * (capacity + BLOCK), LANES), f32),
            pltpu.VMEM((tiles, bucket_rows, LANES), f32),
            pltpu.VMEM((width, row_count), f32),
            pltpu.VMEM((blocks, BLOCK), jnp.int32),
            pltpu.VMEM((3 * blocks + 8, LANES), jnp.int32),
            pltpu.SMEM((3 * blocks + 8, LANES), jnp.int32),
            pltpu.SemaphoreType.DMA((blocks // group,)),
            pltpu.SemaphoreType.DMA((tiles,)),
            pltpu.SemaphoreType.DMA,
        ],
        compiler_params=params(60),
        cost_estimate=cost(10**10, 7 * 10**6),
    )(dest_tile.reshape(2 * blocks, LANES), cells, residual_rows)

    grid_shape = jax.ShapeDtypeStruct((width, height // 2, 2 * across), f32)

    def add(parts, total):
        return pl.pallas_call(
            functools.partial(sum_kernel, width, windows, len(parts), cuts, total is None),
            in_specs=[VMEM] * (len(parts) + (total is not None)),
            out_specs=VMEM,
            out_shape=grid_shape,
            compiler_params=params(40),
            cost_estimate=cost(10**10, 3 * 10**6),
        )(*parts, *(() if total is None else (total,)))

    half = tiles // 2
    order = [half] + list(range(1, half)) + list(range(half + 1, tiles))
    arrived = [
        lax.ppermute(buckets[s], "lon", [(i, i ^ s) for i in range(tiles)]) for s in order
    ]
    state, _ = sweep(state, state, strips, None, False)
    forcing = add([buckets[0]], None)
    each = tiles // 8
    for first in range(0, len(arrived), each):
        forcing = add(arrived[first : first + each], forcing)

    eta, *strips = pl.pallas_call(
        functools.partial(join_kernel, per, chunk_rows),
        grid=(consts // per,),
        in_specs=[
            SMEM,
            fields(2, 0),
            fields(2, 2),
            fields(2, 4),
            plane,
            plane,
            half_re,
            half_im,
        ],
        out_specs=[fields(2, 0)] + strip_specs,
        out_shape=[jax.ShapeDtypeStruct((2,) + state.shape[1:], f32)] + strip_shapes,
        compiler_params=params(32),
        cost_estimate=cost(10**6, 6 * 10**6),
    )(omega, state, state, state, water_depth, ocean_mask, forcing, forcing)
    state, strips = sweep(eta, state, exchange(strips), forcing, True)
    state, _ = sweep(state, state, exchange(strips), forcing, False)
    return state.reshape(tide_state.shape)


def solution(mesh):
    placed = (
        P(None, "lat", "lon"),
        P(None, "lat", "lon"),
        P("lat", "lon"),
        P("lat", "lon"),
        P("lat", "lon"),
        P(None, ("lat", "lon")),
        P(("lat", "lon"), None),
        P(("lat", "lon")),
    )
    return jax.shard_map(
        local, mesh=mesh, in_specs=placed, out_specs=P(None, "lat", "lon"), check_vma=False
    )
```

```python
import functools

import jax
import jax.numpy as jnp
from jax import lax
from jax.experimental import pallas as pl
from jax.experimental.pallas import tpu as pltpu
from jax.sharding import PartitionSpec as P

OMEGAS = [1.405, 1.454, 1.379, 1.458, 0.729, 0.676, 0.725, 0.649]
RELAX = 0.8
LANES = 128
BLOCK = 256
SPAN = 2048
SUM_SPAN = 1024
CUT_BITS = 11
HEAD = 8
MIB = 1 << 20
NT = (((1,), (1,)), ((), ()))
NN = (((1,), (0,)), ((), ()))
VMEM = pl.BlockSpec(memory_space=pltpu.VMEM)
SMEM = pl.BlockSpec(memory_space=pltpu.SMEM)
ANY = pl.BlockSpec(memory_space=pl.ANY)


def iota(shape, dim):
    return lax.broadcasted_iota(jnp.int32, shape, dim)


def params(mib):
    return pltpu.CompilerParams(vmem_limit_bytes=mib * MIB)


def cost(flops, nbytes):
    return pl.CostEstimate(flops=flops, bytes_accessed=nbytes, transcendentals=0)


def rank(tiles, cuts, group, dest_ref, cell_ref, slot_ref, table_ref):
    blocks, block = dest_ref.shape[0] // 2, BLOCK

    def lines(ref):
        return jnp.concatenate(
            [ref[pl.ds(side, blocks, stride=2), :] for side in range(2)], axis=1
        )

    tile = lines(dest_ref) ^ lax.axis_index("lon")
    keys = tile * cuts + ((lines(cell_ref) >> CUT_BITS) & (cuts - 1))
    upper = (iota((block, block), 0) < iota((block, block), 1)).astype(jnp.bfloat16)
    lane = iota((blocks, LANES), 1)
    slot = jnp.zeros((blocks, block), jnp.float32)
    base = jnp.zeros((blocks, 1), jnp.float32)
    counts = jnp.zeros((blocks, LANES), jnp.float32)
    bases = jnp.zeros((blocks, LANES), jnp.float32)
    for key in range(tiles * cuts):
        mine = keys == key
        ones = jnp.where(mine, 1.0, 0.0)
        before = lax.dot_general(
            ones.astype(jnp.bfloat16), upper, NN, preferred_element_type=jnp.float32
        )
        slot = slot + jnp.where(mine, before + base, 0.0)
        count = jnp.sum(ones, axis=1, keepdims=True)
        counts = jnp.where(lane == key, count, counts)
        bases = jnp.where(lane == key, base, bases)
        base = base + count
    lower = (iota((blocks, blocks), 1) < iota((blocks, blocks), 0)).astype(jnp.bfloat16)
    places = lax.dot_general(
        lower, counts.astype(jnp.bfloat16), NN, preferred_element_type=jnp.float32
    )
    total = jnp.broadcast_to(jnp.sum(counts, axis=0, keepdims=True), (8, LANES))
    first = jnp.zeros((8, LANES), jnp.float32)
    for back in range(1, cuts):
        inside = (iota((8, LANES), 1) & (cuts - 1)) >= back
        first = first + jnp.where(inside, pltpu.roll(total, back, 1), 0.0)
    most = jnp.max(counts, axis=1, keepdims=True)
    slot_ref[...] = slot.astype(jnp.int32)
    table_ref[:blocks, :] = jnp.where(lane == LANES - 1, most, counts).astype(jnp.int32)
    table_ref[blocks : 2 * blocks, :] = bases.astype(jnp.int32)
    table_ref[2 * blocks : 3 * blocks, :] = (places + first[0:1]).astype(jnp.int32)
    line, column = iota((8, LANES), 0), iota((8, LANES), 1)
    for part in range(blocks // group):
        largest = jnp.max(most[part * group : (part + 1) * group, :], axis=0, keepdims=True)
        total = jnp.where((line == 1) & (column == part), largest, total)
    table_ref[3 * blocks :, :] = total.astype(jnp.int32)


def bucket_kernel(tiles, cuts, capacity, width, group, *refs):
    dest_ref, cell_ref, rows_any = refs[:3]
    outs = refs[3 : 3 + tiles]
    staged, held, turned, rows_ref, slot_ref, table_held, table_ref = refs[3 + tiles : 10 + tiles]
    read_sem, write_sem, table_sem = refs[10 + tiles :]
    keys = tiles * cuts
    blocks = slot_ref.shape[0]
    windows = capacity // LANES
    room = capacity + BLOCK
    chunk = 32
    inside = iota((chunk, LANES), 0)
    row_of = iota((BLOCK, BLOCK), 0)
    third = iota((16, BLOCK), 0)
    pad = jnp.zeros((LANES - 2 * width - 16, BLOCK), jnp.bfloat16)

    def permute(at, first):
        block = first + at
        slot = slot_ref[pl.ds(block, 1), :]
        cell = jnp.concatenate(
            [cell_ref[pl.ds(2 * block + side, 1), :] for side in range(2)], axis=1
        )
        rows = rows_ref[:, pl.ds(pl.multiple_of(block * BLOCK, BLOCK), BLOCK)]
        high = rows.astype(jnp.bfloat16)
        low = (rows - high.astype(jnp.float32)).astype(jnp.bfloat16)
        cells = jnp.where(
            third == 0, cell >> 7, jnp.where(third == 1, cell & 127, 0)
        ).astype(jnp.float32)
        payload = jnp.concatenate([high, low, cells.astype(jnp.bfloat16), pad], axis=0)
        onehot = jnp.where(row_of == slot, 1.0, 0.0).astype(jnp.bfloat16)
        staged[pl.ds(pl.multiple_of(at * BLOCK, BLOCK), BLOCK), :] = lax.dot_general(
            onehot, payload, NT, preferred_element_type=jnp.float32
        )
        return first

    def move(at, block, key, part):
        count = table_ref[block, key]
        source = at * BLOCK + table_ref[blocks + block, key] + part * chunk
        place = (key // cuts) * room + table_ref[2 * blocks + block, key] + part * chunk
        pltpu.store(
            held.at[pl.ds(place, chunk), :],
            staged[pl.ds(source, chunk), :],
            mask=inside < count - part * chunk,
        )

    def spread(at, first):
        for key in range(keys):
            move(at, first + at, key, 0)
        return first

    def spread_rest(at, first):
        block = first + at

        @pl.when(table_ref[block, LANES - 1] > chunk)
        def _more():
            for key in range(keys):

                def step(part, carry, key=key):
                    move(at, block, key, part)
                    return carry

                lax.fori_loop(1, pl.cdiv(table_ref[block, key], chunk), step, 0)

        return first

    span = group * BLOCK
    reads = [
        pltpu.make_async_copy(
            rows_any.at[:, part * span : (part + 1) * span],
            rows_ref.at[:, part * span : (part + 1) * span],
            read_sem.at[part],
        )
        for part in range(blocks // group)
    ]
    for read in reads:
        read.start()
    rank(tiles, cuts, group, dest_ref, cell_ref, slot_ref, table_held)
    tabled = pltpu.make_async_copy(table_held, table_ref, table_sem)
    tabled.start()
    tabled.wait()
    for part in range(blocks // group):
        reads[part].wait()
        lax.fori_loop(0, group, permute, part * group, unroll=32)
        lax.fori_loop(0, group, spread, part * group, unroll=4)

        @pl.when(table_ref[3 * blocks + 1, part] > chunk)
        def _long(part=part):
            lax.fori_loop(0, group, spread_rest, part * group)

    row, lane = iota((32, LANES), 0), iota((32, LANES), 1)
    joined = jnp.where((row < width) & ((lane == row) | (lane == row + width)), 1.0, 0.0)
    joined = joined + jnp.where((row == width) & (lane == 2 * width), 128.0, 0.0)
    joined = joined + jnp.where((row == width) & (lane == 2 * width + 1), 1.0, 0.0)
    joined = joined.astype(jnp.bfloat16)
    lanes = iota((1, BLOCK), 1)
    writes = []
    for tile in range(tiles):
        out = turned.at[tile]
        sizes = [table_ref[3 * blocks, tile * cuts + cut] for cut in range(cuts)]
        count = functools.reduce(lambda a, b: a + b, sizes)

        def turn(part, carry, tile=tile, count=count, out=out):
            for piece in range(SPAN // BLOCK):
                first = part * SPAN + piece * BLOCK
                block = held[pl.ds(pl.multiple_of(tile * room + first, 8), BLOCK), :]
                both = lax.dot_general(
                    joined, block.astype(jnp.bfloat16), NT, preferred_element_type=jnp.float32
                )
                cells = jnp.where(lanes + first < count, both[width : width + 1], -1.0)
                for side in range(BLOCK // LANES):
                    at = part * (SPAN // LANES) + piece * (BLOCK // LANES) + side
                    cut = slice(side * LANES, (side + 1) * LANES)
                    out[pl.ds(pl.multiple_of(at * width, width), width), :] = both[:width, cut]
                    out[pl.ds(windows * width + at, 1), :] = cells[:, cut]
            return carry

        lax.fori_loop(0, pl.cdiv(count, SPAN), turn, 0)
        line = iota((HEAD, LANES), 0)
        head = jnp.zeros((HEAD, LANES), jnp.int32)
        for cut in range(cuts):
            head = jnp.where(line == cut, sizes[cut], head)
        out[windows * (width + 1) :, :] = head.astype(jnp.float32)
        writes.append(pltpu.make_async_copy(out, outs[tile], write_sem.at[tile]))
        writes[-1].start()
    for write in writes:
        write.wait()


def sum_kernel(width, windows, amount, cuts, fresh, *refs):
    buckets = refs[:amount]
    out = refs[-1]
    half, wide = out.shape[1:]
    high_of = half // cuts
    chunk = SUM_SPAN
    if fresh:
        out[...] = jnp.zeros_like(out)
    else:
        out[...] = refs[amount][...]
    row_of = iota((high_of, chunk), 0)
    col_of = iota((wide, chunk), 0)
    lanes = iota((1, LANES), 1)
    for bucket in buckets:
        top = windows * (width + 1)
        sizes = [
            jnp.max(bucket[top + cut : top + cut + 1, :]).astype(jnp.int32) for cut in range(cuts)
        ]
        total = functools.reduce(lambda a, b: a + b, sizes)
        start = jnp.int32(0)
        for cut in range(cuts):
            first = start // LANES
            start = start + sizes[cut]

            def step(part, carry, bucket=bucket, cut=cut, first=first):
                vals, cells = [], []
                for side in range(chunk // LANES):
                    at = first + part * (chunk // LANES) + side
                    read = jnp.minimum(at, windows - 1)
                    vals.append(bucket[pl.ds(pl.multiple_of(read * width, width), width), :])
                    cell = bucket[pl.ds(windows * width + read, 1), :]
                    cells.append(jnp.where(at * LANES + lanes < total, cell, -1.0))
                rows = jnp.concatenate(vals, axis=1)
                cell = jnp.concatenate(cells, axis=1).astype(jnp.int32)
                grid_row = cell >> 7
                low_row = jnp.where(cell < 0, -1, (grid_row & (half - 1)) - cut * high_of)
                column = (cell & 127) + jnp.where(grid_row >= half, LANES, 0)
                high = rows.astype(jnp.bfloat16)
                low = (rows - high.astype(jnp.float32)).astype(jnp.bfloat16)
                mine = row_of == low_row
                onehot = jnp.where(col_of == column, 1.0, 0.0).astype(jnp.bfloat16)
                left = []
                for channel in range(width):
                    one = slice(channel, channel + 1)
                    left.append(
                        jnp.concatenate(
                            [
                                jnp.where(mine, high[one].astype(jnp.float32), 0.0),
                                jnp.where(mine, low[one].astype(jnp.float32), 0.0),
                            ],
                            axis=1,
                        ).astype(jnp.bfloat16)
                    )
                product = lax.dot_general(
                    jnp.concatenate(left, axis=0),
                    jnp.concatenate([onehot, onehot], axis=1),
                    NT,
                    preferred_element_type=jnp.float32,
                )
                part_of = slice(cut * high_of, (cut + 1) * high_of)
                out[:, part_of, :] += product.reshape(width, high_of, wide)
                return carry

            lax.fori_loop(0, pl.cdiv(start - first * LANES, chunk), step, 0)


def put_edges(strips, k, rows, r0, last_row, fields):
    north, south, west, east = strips
    eta_re, eta_im, east_re, east_im, north_re, north_im = fields
    lane = iota((rows, LANES), 1)
    part = pl.ds(r0, rows)
    for group, field in enumerate((eta_re, eta_im, east_re, east_im)):
        at = group * 8 + k
        west[part, :] = jnp.where(lane == at, pltpu.roll(field, at, 1), west[part, :])
        east[part, :] = jnp.where(lane == at, pltpu.roll(field, at + 1, 1), east[part, :])
    for group, field in enumerate((eta_re, eta_im, north_re, north_im)):
        at = group * 8 + k
        if r0 == 0:
            north[pl.ds(at, 1), :] = field[0:1]
        if r0 + rows == last_row:
            south[pl.ds(at, 1), :] = field[rows - 1 : rows]


def edges_kernel(per, rows, state_ref, depth_ref, *strips):
    for kk in range(per):
        edges_at(pl.program_id(0) * per + kk, kk, rows, state_ref, depth_ref, *strips)


def edges_at(k, kk, rows, state_ref, depth_ref, *strips):
    height = depth_ref.shape[0]
    for r0 in range(0, height, rows):
        part = slice(r0, r0 + rows)
        depth = depth_ref[part, :]
        fields = [state_ref[g, kk, part, :] for g in range(6)]
        fields = fields[:2] + [depth * field for field in fields[2:]]
        put_edges(strips, k, rows, r0, height, fields)


def force(force_ref, channel, r0, rows, half):
    side = r0 // half
    at = r0 % half
    return force_ref[channel, at : at + rows, side * LANES : (side + 1) * LANES]


def join_kernel(per, rows, omega_ref, eta_ref, east_ref, north_ref, depth_ref, ocean_ref, re_ref, im_ref, out_ref, *strips):
    for kk in range(per):
        join_at(pl.program_id(0) * per + kk, kk, rows, omega_ref, eta_ref, east_ref, north_ref, depth_ref, ocean_ref, re_ref, im_ref, out_ref, *strips)


def join_at(k, kk, rows, omega_ref, eta_ref, east_ref, north_ref, depth_ref, ocean_ref, re_ref, im_ref, out_ref, *strips):
    omega = omega_ref[k]
    weight = RELAX / (1.0 + omega * omega)
    height = depth_ref.shape[0]
    for r0 in range(0, height, rows):
        part = slice(r0, r0 + rows)
        depth = depth_ref[part, :]
        ocean = ocean_ref[part, :].astype(jnp.float32) * weight
        f_re = force(re_ref, kk, r0, rows, height // 2)
        f_im = force(im_ref, kk, r0, rows, height // 2)
        eta_re = eta_ref[0, kk, part, :] + ocean * (f_re + f_im * omega)
        eta_im = eta_ref[1, kk, part, :] + ocean * (f_im - f_re * omega)
        out_ref[0, kk, part, :] = eta_re
        out_ref[1, kk, part, :] = eta_im
        fields = [eta_re, eta_im] + [
            depth * ref[g, kk, part, :] for ref in (east_ref, north_ref) for g in range(2)
        ]
        put_edges(strips, k, rows, r0, height, fields)


def sweep_kernel(per, rows, forced, edges, *refs):
    for kk in range(per):
        sweep_at(pl.program_id(0) * per + kk, kk, rows, forced, edges, *refs)


def sweep_at(k, kk, rows, forced, edges, *refs):
    refs = list(refs)
    omega_ref, eta_ref, vel_e_ref, vel_n_ref, pot_ref = refs[:5]
    depth_ref, drag_ref, ocean_ref, turn_ref = refs[5:9]
    north_in, south_in, west_in, east_in = refs[9:13]
    refs = refs[13:]
    if forced:
        re_ref, im_ref = refs[:2]
        refs = refs[2:]
    out_ref = refs[0]
    strips = refs[1:]
    omega = omega_ref[k]
    inv_eta = 1.0 / (1.0 + omega * omega)
    height = depth_ref.shape[0]
    lane = iota((rows, LANES), 1)
    row = iota((rows, LANES), 0)

    def dlon(q, group, r0):
        at = group * 8 + k
        part = slice(r0, r0 + rows)
        left = pltpu.roll(q, 1, 1)
        right = pltpu.roll(q, LANES - 1, 1)
        w = pltpu.roll(west_in[part, :], (LANES - at) % LANES, 1)
        e = pltpu.roll(east_in[part, :], LANES - 1 - at, 1)
        return (jnp.where(lane == LANES - 1, e, right) - jnp.where(lane == 0, w, left)) * 0.5

    def shifted(q, first, last, group, r0):
        at = group * 8 + k
        above = first if r0 > 0 else north_in[pl.ds(at, 1), :]
        below = last if r0 + rows < height else south_in[pl.ds(at, 1), :]
        up = jnp.where(row == 0, above, pltpu.roll(q, 1, 0))
        down = jnp.where(row == rows - 1, below, pltpu.roll(q, rows - 1, 0))
        return (down - up) * 0.5

    for r0 in range(0, height, rows):
        part = slice(r0, r0 + rows)
        before = slice(max(r0 - 1, 0), max(r0 - 1, 0) + 1)
        after = slice(min(r0 + rows, height - 1), min(r0 + rows, height - 1) + 1)
        depth = depth_ref[part, :]
        diag = 1.0 + drag_ref[part, :]
        ocean = ocean_ref[part, :].astype(jnp.float32)
        turn = turn_ref[part, :]
        inv = 1.0 / (diag * diag + omega * omega)
        eta = [eta_ref[g, kk, part, :] for g in range(2)]
        east = [vel_e_ref[g, kk, part, :] for g in range(2)]
        north = [vel_n_ref[g, kk, part, :] for g in range(2)]
        pot = [pot_ref[g, kk, part, :] for g in range(6)]
        flux = []
        grad_lat = []
        for g in range(2):
            hn = depth * north[g]
            hn_first = depth_ref[before, :] * vel_n_ref[g, kk, before, :]
            hn_last = depth_ref[after, :] * vel_n_ref[g, kk, after, :]
            flux.append(
                dlon(depth * east[g], 2 + g, r0) + shifted(hn, hn_first, hn_last, 2 + g, r0)
            )
            grad_lat.append(
                shifted(eta[g], eta_ref[g, kk, before, :], eta_ref[g, kk, after, :], g, r0)
            )
        grad_lon = [dlon(eta[g], g, r0) for g in range(2)]
        res_re = pot[0] - (eta[0] - omega * eta[1] + flux[0])
        res_im = pot[1] - (eta[1] + omega * eta[0] + flux[1])
        if forced:
            res_re = res_re + force(re_ref, kk, r0, rows, height // 2)
            res_im = res_im + force(im_ref, kk, r0, rows, height // 2)
        weight = ocean * RELAX
        new = [
            ocean * eta[0] + weight * ((res_re + res_im * omega) * inv_eta),
            ocean * eta[1] + weight * ((res_im - res_re * omega) * inv_eta),
        ]
        scaled = weight * inv
        for own, other, grad, at, sign in (
            (east, north, grad_lon, 2, -1.0),
            (north, east, grad_lat, 4, 1.0),
        ):
            spun = [sign * (turn * other[g]) for g in range(2)]
            res_re = pot[at] - (diag * own[0] - omega * own[1] + spun[0] + grad[0])
            res_im = pot[at + 1] - (diag * own[1] + omega * own[0] + spun[1] + grad[1])
            new.append(ocean * own[0] + scaled * (res_re * diag + res_im * omega))
            new.append(ocean * own[1] + scaled * (res_im * diag - res_re * omega))
        for g in range(6):
            out_ref[g, kk, part, :] = new[g]
        if edges:
            put_edges(strips, k, rows, r0, height, new[:2] + [depth * q for q in new[2:]])


def local(
    tide_state, potential, water_depth, drag_coeff, ocean_mask, residual_rows, dest_tile, dest_cell
):
    f32 = jnp.float32
    tiles = lax.axis_size("lon")
    lats = lax.axis_size("lat")
    width, row_count = residual_rows.shape
    capacity = 2 * row_count // tiles
    height, across = water_depth.shape
    consts = tide_state.shape[0] // 6
    blocks = row_count // BLOCK
    windows = capacity // LANES
    cuts = max(1, min(4, 32 // tiles))
    cells = dest_cell.reshape(2 * blocks, LANES)
    bucket_rows = windows * (width + 1) + HEAD

    group = min(32, blocks)
    omega = jnp.asarray(OMEGAS, f32)
    row_ids = lax.axis_index("lat") * height + jnp.arange(height, dtype=jnp.int32)
    lat_pos = (row_ids.astype(f32) + 0.5) / (height * lats) - 0.5
    turn = jnp.broadcast_to((0.5 * jnp.sin(jnp.pi * lat_pos))[:, None], (height, across))

    state = tide_state.reshape(6, consts, height, across)
    pot = potential.reshape(6, consts, height, across)
    chunk_rows, per = 64, 4

    def fields(count, first):
        return pl.BlockSpec((count, per, height, across), lambda k: (first // count, k, 0, 0))

    plane = pl.BlockSpec((height, across), lambda k: (0, 0))
    flat = pl.BlockSpec((4 * consts, across), lambda k: (0, 0))
    half_re = pl.BlockSpec((per, height // 2, 2 * across), lambda k: (k, 0, 0))
    half_im = pl.BlockSpec((per, height // 2, 2 * across), lambda k: (consts // per + k, 0, 0))
    strip_specs = [flat, flat, plane, plane]
    strip_shapes = [jax.ShapeDtypeStruct((4 * consts, across), f32)] * 2 + [
        jax.ShapeDtypeStruct((height, across), f32)
    ] * 2
    state_shape = jax.ShapeDtypeStruct(state.shape, f32)

    def exchange(strips):
        north, south, west, east = strips
        return (
            lax.ppermute(south, "lat", [(i, i + 1) for i in range(lats - 1)]),
            lax.ppermute(north, "lat", [(i + 1, i) for i in range(lats - 1)]),
            lax.ppermute(east, "lon", [(i, (i + 1) % tiles) for i in range(tiles)]),
            lax.ppermute(west, "lon", [((i + 1) % tiles, i) for i in range(tiles)]),
        )

    def sweep(eta, vel, strips, forcing, edges):
        forced = forcing is not None
        out = pl.pallas_call(
            functools.partial(sweep_kernel, per, chunk_rows, forced, edges),
            grid=(consts // per,),
            in_specs=[SMEM, fields(2, 0), fields(2, 2), fields(2, 4), fields(6, 0)]
            + [plane] * 4
            + strip_specs
            + ([half_re, half_im] if forced else []),
            out_specs=[fields(6, 0)] + (strip_specs if edges else []),
            out_shape=[state_shape] + (strip_shapes if edges else []),
            compiler_params=params(32),
            cost_estimate=cost(16 * 10**6, 9 * 10**6),
        )(
            omega, eta, vel, vel, pot, water_depth, drag_coeff, ocean_mask, turn, *strips,
            *((forcing, forcing) if forced else ()),
        )
        return out[0], out[1:]

    strips = pl.pallas_call(
        functools.partial(edges_kernel, per, chunk_rows),
        grid=(consts // per,),
        in_specs=[fields(6, 0), plane],
        out_specs=strip_specs,
        out_shape=strip_shapes,
        compiler_params=params(32),
        cost_estimate=cost(10**6, 3 * 10**6),
    )(state, water_depth)
    strips = exchange(strips)


    buckets = pl.pallas_call(
        functools.partial(bucket_kernel, tiles, cuts, capacity, width, group),
        in_specs=[VMEM, VMEM, ANY],
        out_specs=[ANY] * tiles,
        out_shape=[jax.ShapeDtypeStruct((bucket_rows, LANES), f32)] * tiles,
        scratch_shapes=[
            pltpu.VMEM(((group + 1) * BLOCK, LANES), f32),
            pltpu.VMEM((tiles * (capacity + BLOCK), LANES), f32),
            pltpu.VMEM((tiles, bucket_rows, LANES), f32),
            pltpu.VMEM((width, row_count), f32),
            pltpu.VMEM((blocks, BLOCK), jnp.int32),
            pltpu.VMEM((3 * blocks + 8, LANES), jnp.int32),
            pltpu.SMEM((3 * blocks + 8, LANES), jnp.int32),
            pltpu.SemaphoreType.DMA((blocks // group,)),
            pltpu.SemaphoreType.DMA((tiles,)),
            pltpu.SemaphoreType.DMA,
        ],
        compiler_params=params(60),
        cost_estimate=cost(10**10, 7 * 10**6),
    )(dest_tile.reshape(2 * blocks, LANES), cells, residual_rows)

    grid_shape = jax.ShapeDtypeStruct((width, height // 2, 2 * across), f32)

    def add(parts, total):
        return pl.pallas_call(
            functools.partial(sum_kernel, width, windows, len(parts), cuts, total is None),
            in_specs=[VMEM] * (len(parts) + (total is not None)),
            out_specs=VMEM,
            out_shape=grid_shape,
            compiler_params=params(40),
            cost_estimate=cost(10**10, 3 * 10**6),
        )(*parts, *(() if total is None else (total,)))

    half = tiles // 2
    order = [half] + list(range(1, half)) + list(range(half + 1, tiles))
    arrived = [
        lax.ppermute(buckets[s], "lon", [(i, i ^ s) for i in range(tiles)]) for s in order
    ]
    state, _ = sweep(state, state, strips, None, False)
    forcing = add([buckets[0]], None)
    each = tiles // 8
    ends = [0, each, 2 * each, 3 * each, 5 * each, 6 * each, len(arrived)]
    for first, last in zip(ends, ends[1:]):
        forcing = add(arrived[first:last], forcing)

    eta, *strips = pl.pallas_call(
        functools.partial(join_kernel, per, chunk_rows),
        grid=(consts // per,),
        in_specs=[
            SMEM,
            fields(2, 0),
            fields(2, 2),
            fields(2, 4),
            plane,
            plane,
            half_re,
            half_im,
        ],
        out_specs=[fields(2, 0)] + strip_specs,
        out_shape=[jax.ShapeDtypeStruct((2,) + state.shape[1:], f32)] + strip_shapes,
        compiler_params=params(32),
        cost_estimate=cost(10**6, 6 * 10**6),
    )(omega, state, state, state, water_depth, ocean_mask, forcing, forcing)
    state, strips = sweep(eta, state, exchange(strips), forcing, True)
    state, _ = sweep(state, state, exchange(strips), forcing, False)
    return state.reshape(tide_state.shape)


def solution(mesh):
    placed = (
        P(None, "lat", "lon"),
        P(None, "lat", "lon"),
        P("lat", "lon"),
        P("lat", "lon"),
        P("lat", "lon"),
        P(None, ("lat", "lon")),
        P(("lat", "lon"), None),
        P(("lat", "lon")),
    )
    return jax.shard_map(
        local, mesh=mesh, in_specs=placed, out_specs=P(None, "lat", "lon"), check_vma=False
    )
```
